256 devices in a mesh: dp: 16 (over z, core), ep: 16 (over y, x).
Axes of the slice: x: 4, y: 4, z: 8, core: 2. Of those that a mesh axis runs over, the one named last changes fastest.
Arguments:
- latent_cache: bfloat16 [64, 8192, 576], P('dp', 'ep'), may hold values from -6 to 6, as said below
- lengths: int32 [64], replicated, may hold values from 2 to 8192, as said below
- queries: bfloat16 [2, 64, 128, 576], P(None, 'dp'), may hold values from -12 to 12
- fresh_latent: bfloat16 [2, 64, 576], P(None, 'dp'), may hold values from -6 to 6
- leaving: int32 [16], replicated, may hold values from 0 to 3
- target: int32 [16], replicated, may hold values from 0 to 15, as said below
- value_weight: bfloat16 [128, 512, 128], P('ep'), may hold values from -0.25 to 0.25
- output_weight: bfloat16 [128, 128, 7168], P('ep', 'dp'), may hold values from -0.0625 to 0.0625
- residual_stream: bfloat16 [2, 64, 7168], replicated, may hold values from -17 to 17
- norm_gain: bfloat16 [7168], replicated, may hold values from 0.099609375 to 1.8984375
- expert_ids: int32 [2, 64, 8], replicated, may hold values from 0 to 15, all different within a row
- gate_codes: int32 [2, 64, 8], replicated, may hold values from 1 to 65535
- gate_weight: bfloat16 [16, 7168, 2048], P('ep', None, 'dp'), may hold values from -0.0625 to 0.0625
- up_weight: bfloat16 [16, 7168, 2048], P('ep', None, 'dp'), may hold values from -0.0625 to 0.0625
- down_weight: bfloat16 [16, 2048, 7168], P('ep', 'dp'), may hold values from -0.1875 to 0.1875
Outputs:
- mixed: bfloat16 [2, 64, 7168], P(None, 'dp', 'ep')
The draws below stay inside these ranges and needn't reach their ends.
Inputs may be any that keep to these rules, and one draw needn't show every extreme that they name: `latent_cache`: entries at positions at or beyond a slot's length are never read. `lengths`: one session has exactly 8192 cached positions. A permutation of the ranks without a fixed point: rank r hands the session of slot leaving[r] to rank target[r], which puts it in its own slot leaving[target[r]].
All inputs are finite; a program needn't handle non-finite values.
Results may differ from the reference program's by a relative error of at most 0.015.
Values may be sent and summed in bfloat16 or wider, within the bound.
A program may use at most 128 MiB of HBM per device.

```python
import jax
import jax.numpy as jnp
from jax import lax

D = 7168
H = 128
LAT = 512
VD = 128
FF = 2048
SLOTS = 4
CAP_DEV = 512
RANKS = 16
S = 64
CAP = 8192
LATW = 576
EXPERTS = 16
TOP = 8
N_EP = 16


def draw_latent_cache(key, part):
    key = jax.random.fold_in(key, 11)
    drawn = jax.random.truncated_normal(key, -6.0, 6.0, (S, CAP, LATW), jnp.float32)
    return drawn.astype(jnp.bfloat16)


def draw_queries(key, part):
    key = jax.random.fold_in(key, 12)
    drawn = 2.0 * jax.random.truncated_normal(key, -6.0, 6.0, (2, S, H, LATW), jnp.float32)
    return drawn.astype(jnp.bfloat16)


def draw_lengths(key, part):
    key = jax.random.fold_in(key, 13)
    key_lengths, key_full = jax.random.split(key)
    drawn = jax.random.randint(key_lengths, (S,), 2, CAP + 1)
    full_slot = jax.random.randint(key_full, (), 0, S)
    return jnp.where(jnp.arange(S) == full_slot, CAP, drawn).astype(jnp.int32)


def draw_target(key, part):
    key = jax.random.fold_in(key, 14)
    cycle = jax.random.permutation(key, RANKS).astype(jnp.int32)
    following = jnp.roll(cycle, -1)
    return jnp.zeros((RANKS,), jnp.int32).at[cycle].set(following)


def draw_residual_stream(key, part):
    key = jax.random.fold_in(key, 15)
    drawn = jax.random.truncated_normal(key, -6.0, 6.0, (2, S, D), jnp.float32)
    return drawn.astype(jnp.bfloat16)


def touch_ends(result, own_key, low, high):
    longest = result.shape.index(max(result.shape))
    spots = []
    for shift in (0, 1):
        where = [jax.random.randint(jax.random.fold_in(own_key, axis), (), 0, length) for axis, length in enumerate(result.shape)]
        where[longest] = (where[longest] + shift) % result.shape[longest]
        spots.append(tuple(where))
    return result.at[spots[0]].set(low).at[spots[1]].set(high)


def raised(entries, key, source, target, shards_of, factor):
    owner, partner = [(jnp.arange(entries.shape[dim]) // (entries.shape[dim] // shards_of)).reshape([-1 if axis == dim else 1 for axis in range(entries.ndim)]) for dim in (source, target)]
    chosen = jax.random.permutation(key, shards_of)[partner]
    strong = (owner == chosen) | (owner == (partner + shards_of // 2) % shards_of)
    return jnp.where(strong, factor * entries, entries)


def steps_of(own_key, extent, cuts, smallest, top_value):
    factor_of = 1.0
    for dim, parts in cuts:
        steps = jax.random.uniform(jax.random.fold_in(jax.random.fold_in(own_key, 6), dim), (parts,), jnp.float32, smallest / len(cuts), top_value / len(cuts))
        factor_of = factor_of * jnp.repeat(jnp.exp(steps), extent[dim] // parts).reshape((-1,) + (1,) * (len(extent) - 1 - dim))
    return factor_of


def choose_distinct(rng, rows, number_of, top, lift):
    sequence = jax.random.permutation(jax.random.fold_in(rng, 1), number_of)
    boost = sequence
    for power in range(3):
        boost = boost * boost // number_of
    boost = boost * lift // number_of
    tickets = jax.random.randint(jax.random.fold_in(rng, 2), (rows, number_of), 0, 4096) + boost
    holders = jax.random.permutation(jax.random.fold_in(rng, 3), rows)[jnp.arange(number_of) % rows]
    tickets = jnp.where(jnp.arange(rows)[:, None] == holders[None, :], 1 << 14, tickets)
    priority = tickets * number_of + jnp.arange(number_of)
    return lax.top_k(priority.astype(jnp.int32), top)[1].astype(jnp.int32)


def normal_values(key, dims, spread, most, pieces=(), kind=jnp.bfloat16):
    values = spread * jax.random.normal(key, dims, jnp.float32)
    if pieces:
        values = values * steps_of(key, dims, pieces, -0.22, 0.18)
    return jnp.clip(values, -most, most).astype(kind)


def heavy_noise(stream_key, dims, width, reach, cuts, heavy, held_as=jnp.bfloat16):
    values = width * jax.random.normal(stream_key, dims, jnp.float32)
    if cuts:
        values = values * steps_of(stream_key, dims, cuts, -0.22, 0.18)
    return jnp.clip(raised(values, jax.random.fold_in(stream_key, 3), *heavy), -reach, reach).astype(held_as)


def setup_inputs(seed: int = 0) -> dict:
    key_of = jax.random.split(jax.random.key(seed), 16)
    return {
        "latent_cache": draw_latent_cache(jax.random.fold_in(key_of[15], 71), 0),
        "lengths": draw_lengths(jax.random.fold_in(key_of[15], 71), 0),
        "queries": draw_queries(jax.random.fold_in(key_of[15], 71), 0),
        "fresh_latent": normal_values(key_of[3], (2, S, LATW), 1.0, 6.0, ((1, 16),)),
        "leaving": touch_ends(jax.random.randint(key_of[4], (RANKS,), 0, SLOTS), jax.random.fold_in(key_of[4], 1), 0, SLOTS - 1).astype(jnp.int32),
        "target": draw_target(jax.random.fold_in(key_of[15], 71), 0),
        "value_weight": normal_values(key_of[6], (H, LAT, VD), LAT ** -0.5, 0.25, ((0, 16),)),
        "output_weight": heavy_noise(key_of[7], (H, VD, D), (H * VD) ** -0.5, 0.0625, ((0, 16), (1, 16)), (1, 2, 16, 2.0)),
        "residual_stream": draw_residual_stream(jax.random.fold_in(key_of[15], 71), 0),
        "norm_gain": jnp.clip(1.0 + 0.18 * jax.random.normal(key_of[9], (D,), jnp.float32), 0.099609375, 1.8984375).astype(jnp.bfloat16),
        "expert_ids": choose_distinct(key_of[10], 2 * S, EXPERTS, TOP, 4096).reshape((2, S, TOP)),
        "gate_codes": touch_ends(jax.random.randint(key_of[11], (2, S, TOP), 1, 65536), jax.random.fold_in(key_of[11], 1), 1, 65535).astype(jnp.int32),
        "gate_weight": normal_values(key_of[12], (EXPERTS, D, FF), D ** -0.5, 0.0625, ((0, 16), (2, 16))),
        "up_weight": normal_values(key_of[13], (EXPERTS, D, FF), D ** -0.5, 0.0625, ((0, 16), (2, 16))),
        "down_weight": heavy_noise(key_of[14], (EXPERTS, FF, D), FF ** -0.5, 0.1875, ((0, 16), (1, 16)), (1, 2, 16, 2.0)),
    }


SCORE_SCALE = 192.0 ** (-0.5)
ROUTE_SCALE = 2.5
NORM_EPS = 1e-06
MASKED = -1e+30

def session_order(leaving, target):
    positions = jnp.arange(S, dtype=jnp.int32)
    arrive = target * SLOTS + leaving[target]
    depart = jnp.arange(RANKS, dtype=jnp.int32) * SLOTS + leaving
    return positions.at[arrive].set(depart)

def attend_slot(query_rows, cache_rows, length, fresh_keys):
    blocks = cache_rows.reshape(N_EP, CAP_DEV, LATW).astype(jnp.float32)
    query_wide = query_rows.astype(jnp.float32)
    scores = jnp.einsum('hc,btc->bht', query_wide, blocks) * SCORE_SCALE
    positions = jnp.arange(CAP, dtype=jnp.int32).reshape(N_EP, CAP_DEV)
    live_mask = (positions < length)[:, None, :]
    masked = jnp.where(live_mask, scores, MASKED)
    block_peak = lax.optimization_barrier(jnp.max(masked, axis=2))
    raw_weights = jnp.where(live_mask, jnp.exp(masked - block_peak[..., None]), 0.0)
    block_sum = lax.optimization_barrier(jnp.sum(raw_weights, axis=2))
    block_weights = raw_weights.astype(jnp.bfloat16).astype(jnp.float32)
    block_values = jnp.einsum('bht,btl->bhl', block_weights, blocks[:, :, :LAT])
    fresh_scores = jnp.dot(query_rows, fresh_keys.T, preferred_element_type=jnp.float32) * SCORE_SCALE
    best_score = jnp.maximum(lax.optimization_barrier(jnp.max(block_peak, axis=0)), lax.optimization_barrier(jnp.max(fresh_scores, axis=1)))
    block_scale = jnp.exp(block_peak - best_score[None, :])
    fresh_weight = jnp.exp(fresh_scores - best_score[:, None])
    fresh_values = fresh_keys[:, :LAT].astype(jnp.float32)
    numerator = lax.optimization_barrier(jnp.sum(block_scale[..., None] * block_values, axis=0)) + jnp.dot(fresh_weight, fresh_values, precision=lax.Precision.HIGHEST)
    denominator = lax.optimization_barrier(jnp.sum(block_scale * block_sum, axis=0)) + lax.optimization_barrier(jnp.sum(fresh_weight, axis=1))
    return numerator / denominator[:, None]

def attend_all(queries_step, latent_cache, lengths, fresh_keys, new_order):

    def attend_index(position):
        before = new_order[position]
        return attend_slot(queries_step[position], latent_cache[before], lengths[before], fresh_keys[position])
    return lax.map(attend_index, jnp.arange(S, dtype=jnp.int32))

def layer_step(attended, residual_rows, value_weight, output_weight, norm_gain, chosen, codes, gate_weight, up_weight, down_weight):
    latent = attended.astype(jnp.bfloat16)
    values = jnp.einsum('shl,hlv->shv', latent.astype(jnp.float32), value_weight.astype(jnp.float32)).astype(jnp.bfloat16)
    attn_sum = jnp.dot(values.reshape(S, H * VD), output_weight.reshape(H * VD, D), preferred_element_type=jnp.float32)
    hidden = residual_rows.astype(jnp.float32) + attn_sum
    scale_rows = lax.rsqrt(lax.optimization_barrier(jnp.mean(hidden * hidden, axis=1, keepdims=True)) + NORM_EPS)
    normed = (hidden * scale_rows * norm_gain.astype(jnp.float32)).astype(jnp.bfloat16)
    code_wide = codes.astype(jnp.float32)
    shares = code_wide / lax.optimization_barrier(jnp.sum(code_wide, axis=1, keepdims=True)) * ROUTE_SCALE
    expert_axis = jnp.arange(EXPERTS, dtype=jnp.int32)
    route_weight = lax.optimization_barrier(jnp.sum(jnp.where(chosen[:, :, None] == expert_axis[None, None, :], shares[:, :, None], 0.0), axis=1))

    def add_expert(running, expert):
        gate_proj = jnp.dot(normed, gate_weight[expert], preferred_element_type=jnp.float32)
        up_proj = jnp.dot(normed, up_weight[expert], preferred_element_type=jnp.float32)
        activated = (jax.nn.silu(gate_proj) * up_proj).astype(jnp.bfloat16)
        expert_out = jnp.dot(activated, down_weight[expert], preferred_element_type=jnp.float32)
        column = lax.dynamic_slice_in_dim(route_weight, expert, 1, 1)
        return (running + column * expert_out, None)
    routed, _ = lax.scan(add_expert, jnp.zeros((S, D), jnp.float32), expert_axis)
    return (hidden + routed).astype(jnp.bfloat16)

def reference(latent_cache, lengths, queries, fresh_latent, leaving, target, value_weight, output_weight, residual_stream, norm_gain, expert_ids, gate_codes, gate_weight, up_weight, down_weight):
    new_order = session_order(leaving, target)
    identity_order = jnp.arange(S, dtype=jnp.int32)
    fresh_one = fresh_latent[0][:, None, :]
    fresh_two = jnp.stack([fresh_latent[0][new_order], fresh_latent[1]], axis=1)
    attended_one = attend_all(queries[0], latent_cache, lengths, fresh_one, identity_order)
    attended_two = attend_all(queries[1], latent_cache, lengths, fresh_two, new_order)
    mixed_one = layer_step(attended_one, residual_stream[0], value_weight, output_weight, norm_gain, expert_ids[0], gate_codes[0], gate_weight, up_weight, down_weight)
    mixed_two = layer_step(attended_two, residual_stream[1], value_weight, output_weight, norm_gain, expert_ids[1], gate_codes[1], gate_weight, up_weight, down_weight)
    return jnp.stack([mixed_one, mixed_two])
```

```python
import functools

import jax
import jax.numpy as jnp
from jax import lax
from jax.experimental import pallas as pl
from jax.experimental.pallas import tpu as pltpu
from jax.sharding import PartitionSpec as P

MESH = pl.DeviceIdType.MESH
SCORE_SCALE = 192.0 ** (-0.5)
ROUTE_SCALE = 2.5
NORM_EPS = 1e-06
MASKED = -1e30
LAT = 512
BF = jnp.bfloat16
F32 = jnp.float32


def iota(shape, dim):
    return lax.broadcasted_iota(jnp.int32, shape, dim)


def dot(a, b, ca=1, cb=0):
    return lax.dot_general(a, b, (((ca,), (cb,)), ((), ())), preferred_element_type=F32)


def loop(lo, hi, fn):
    lax.fori_loop(lo, hi, lambda i, c: (fn(i), c)[1], 0)


def kernel(
    DP, EP,
    lengths, leaving, target, fresh, ids, codes, gain, resid,
    cache_h, q_h, vw_h, ow_h, gate_h, up_h, down_h,
    out,
    q1v, q2v, cv, vw, ow, gu, dn,
    a1s, a1r, a2s, a2r, fk,
    bs, bt, br, btr, sc, lat,
    cs, cr,
    pc, pr, xs, xr, zs, zr,
    pc2, pr2, xs2, xr2, zs2, zr2,
    gs, gr, hb, rw,
    ld, sa1, ra1, sa2, ra2, sb, rb, st, rt, scs, rcs,
    s1c, r1c, s1x, r1x, s1z, r1z,
    s2c, r2c, s2x, r2x, s2z, r2z,
    sgz, rgz, sgx, rgx, sgc, rgc,
):
    NZ = DP // 2
    SL = 4
    HP = vw.shape[0]
    VD = vw.shape[2]
    VC = VD // DP
    ROWS = DP * 8
    HALF = ROWS // 2
    BW = gain.shape[1]
    LW = cv.shape[1]
    T = cv.shape[2]
    HEADS = q1v.shape[2]
    PIECE = a2s.shape[0]
    dp = lax.axis_index("dp")
    ep = lax.axis_index("ep")
    z = dp // 2
    core = dp % 2

    def to_dp(k):
        return (dp + k) % DP

    def to_ep(k):
        return (ep + k) % EP

    def remote(src, dst, s, r, d, e):
        return pltpu.make_async_remote_copy(
            src_ref=src, dst_ref=dst, send_sem=s, recv_sem=r, device_id=(d, e), device_id_type=MESH
        )

    def local(src, dst, k):
        return pltpu.make_async_copy(src, dst, ld.at[k])

    loads = [local(q_h.at[1], q2v, 0), local(q_h.at[0], q1v, 1)]
    loads += [local(cache_h.at[s], cv.at[s], 2 + s) for s in range(SL)]
    loads += [
        local(vw_h, vw, 6),
        local(ow_h, ow, 7),
        local(gate_h, gu.at[:, pl.ds(0, 128)], 8),
        local(up_h, gu.at[:, pl.ds(128, 128)], 9),
        local(down_h, dn, 10),
    ]
    for c in loads:
        c.start()

    barrier = pltpu.get_barrier_semaphore()
    loop(1, DP, lambda k: pl.semaphore_signal(barrier, inc=1, device_id=(to_dp(k), ep), device_id_type=MESH))
    loop(1, EP, lambda k: pl.semaphore_signal(barrier, inc=1, device_id=(dp, to_ep(k)), device_id_type=MESH))

    lv = leaving[dp]
    f0 = fresh[0].astype(F32)
    f1 = fresh[1].astype(F32)
    frow = jnp.sum(jnp.where(iota(f1.shape, 0) == lv, f1, 0.0), axis=0, keepdims=True)
    frow = jnp.concatenate([frow, jnp.zeros((1, 640 - LW), F32)], axis=1)
    fpieces = [frow[:, 128 * i : 128 * (i + 1)] for i in range(5)]
    loads[0].wait()
    a1s[0:LW, 0:HEADS] = q2v[lv]
    a1s[LW : LW + 16] = jnp.concatenate(fpieces + [jnp.zeros((11, 128), F32)], axis=0).astype(BF)
    a1s[LW + 16 :] = jnp.zeros((a1s.shape[0] - LW - 16, 128), BF)
    mine = pl.ds(pl.multiple_of(ep * PIECE, 16), PIECE)
    a1r[dp] = a1s[mine]
    pl.semaphore_wait(barrier, DP + EP - 2)

    def a1(k):
        d = to_dp(k)
        return remote(a1s.at[mine], a1r.at[dp], sa1.at[d], ra1.at[dp], d, ep)

    loop(1, DP, lambda k: a1(k).start())

    def attend(q, s, live_fresh):
        kt = cv[s]
        score = dot(q, kt, 0, 0) * SCORE_SCALE
        pos = ep * T + iota(score.shape, 1)
        live = pos < lengths[dp * SL + s]
        fkeys = fk[...]
        fscore = dot(q, fkeys, 0, 1) * SCORE_SCALE
        score = jnp.where(live, score, MASKED)
        fscore = jnp.where(live_fresh, fscore, MASKED)
        peak = jnp.maximum(
            jnp.max(score, axis=1, keepdims=True), jnp.max(fscore, axis=1, keepdims=True)
        )
        w = jnp.where(live, jnp.exp(score - peak), 0.0)
        fw = jnp.where(live_fresh, jnp.exp(fscore - peak), 0.0)
        total = jnp.sum(w, axis=1, keepdims=True) + jnp.sum(fw, axis=1, keepdims=True)
        v = dot(w.astype(BF), kt[:LAT], 1, 1) + dot(fw.astype(BF), fkeys[:, :LAT])
        return peak, total, v

    group = iota((HEADS, 128), 1) >> 4

    def attend_step(k, query_of, live_of):
        stat = jnp.zeros((HEADS, 128), F32)
        for p in range(SL // 2):
            both = []
            for s in (2 * p, 2 * p + 1):
                peak, total, v = attend(query_of(s), s, live_of(s))
                stat = jnp.where(group == 2 * s, peak, jnp.where(group == 2 * s + 1, total, stat))
                both.append(v.reshape(EP, HP, LAT))
            bs[k, :, 16 * p : 16 * p + 16, :] = jnp.concatenate(both, axis=1).astype(BF)
        bt[k] = stat.reshape(EP, HP, 128)
        br[k, ep] = bs[k, ep]
        btr[k, ep] = bt[k, ep]

    def b_copy(k, i):
        e = to_ep(i)
        return remote(bs.at[k, e], br.at[k, ep], sb.at[k, e], rb.at[k, ep], dp, e)

    def t_copy(k, i):
        e = to_ep(i)
        return remote(bt.at[k, e], btr.at[k, ep], st.at[k, e], rt.at[k, ep], dp, e)

    def b_wait(k, i):
        e = to_ep(i)
        remote(bs.at[k, e], br.at[k, e], sb.at[k, e], rb.at[k, e], dp, e).wait_recv()
        remote(bt.at[k, e], btr.at[k, e], st.at[k, e], rt.at[k, e], dp, e).wait_recv()

    def b_start(k):
        def go(i):
            t_copy(k, i).start()
            b_copy(k, i).start()

        loop(1, EP, go)

    fcol = iota((1, 16), 1)
    at_zero = ep == 0
    fk[...] = jnp.concatenate([f0, f1, jnp.zeros((8, LW), F32)], axis=0).astype(BF)
    loads[1].wait()
    for s in range(SL):
        loads[2 + s].wait()
    attend_step(0, lambda s: q1v[s], lambda s: (fcol == s) & at_zero)

    def a1_wait(k):
        d = to_dp(k)
        remote(a1s.at[mine], a1r.at[d], sa1.at[d], ra1.at[d], d, ep).wait_recv()

    loop(1, DP, a1_wait)
    piece = a1r[target[dp]]
    a2s[...] = piece
    a2r[mine] = piece

    def a2(k):
        e = to_ep(k)
        return remote(a2s, a2r.at[mine], sa2.at[e], ra2.at[ep], dp, e)

    def a2_wait(k):
        e = to_ep(k)
        rows = pl.ds(pl.multiple_of(e * PIECE, 16), PIECE)
        remote(a2s, a2r.at[rows], sa2.at[e], ra2.at[e], dp, e).wait_recv()

    loop(1, EP, lambda k: a2(k).start())
    b_start(0)

    row = iota((ROWS, 2 * SL * DP), 0)
    col = iota((ROWS, 2 * SL * DP), 1)
    half_bits = HALF.bit_length() - 1
    r_core = row >> half_bits
    r_z = (row >> 3) & (NZ - 1)
    r_step = (row >> 2) & 1
    slot = (r_z * 2 + r_core) * SL + (row & 3)
    held = slot
    for r in range(DP):
        t = target[r]
        held = jnp.where(slot == t * SL + leaving[t], r * SL + leaving[r], held)
    place = (r_step * (SL * DP) + jnp.where(r_step == 1, held, slot)) == col
    code = codes[...].astype(F32)
    share = code / jnp.sum(code, axis=1, keepdims=True) * ROUTE_SCALE
    weight = jnp.sum(jnp.where(ids[...] == ep, share, 0.0), axis=1)
    weight = jnp.concatenate([weight[0:1], weight[1:2]], axis=1)
    own_place = (r_step * (SL * DP) + slot) == col
    rw[...] = jnp.broadcast_to(
        jnp.sum(jnp.where(own_place, weight, 0.0), axis=1, keepdims=True), (ROWS, 128)
    )
    place = jnp.where(place, 1.0, 0.0).astype(BF)

    loop(1, EP, a2_wait)
    moved_f = a2r[LW : LW + 16].astype(F32)
    moved_f = jnp.concatenate([moved_f[i : i + 1] for i in range(5)], axis=1)[:, :LW]
    fk[...] = jnp.concatenate([f0, f1, moved_f, jnp.zeros((7, LW), F32)], axis=0).astype(BF)
    moved_q = a2r[0:LW, 0:HEADS]
    attend_step(
        1,
        lambda s: jnp.where(lv == s, moved_q, q2v[s]),
        lambda s: ((fcol == s) | (fcol == jnp.where(lv == s, 8, 4 + s))) & at_zero,
    )
    b_start(1)

    head_of = iota((SL * HP, VD), 0) & (HP - 1)

    def c_copy(k, i):
        d = to_dp(i)
        return remote(cs.at[k], cr.at[k, dp], scs.at[k, d], rcs.at[k, dp], d, ep)

    def c_wait(k, i):
        d = to_dp(i)
        remote(cs.at[k], cr.at[k, d], scs.at[k, d], rcs.at[k, d], d, ep).wait_recv()

    def merge(k):
        loop(1, EP, lambda i: b_wait(k, i))
        stats = btr[k]
        w = jnp.exp(stats - jnp.max(stats, axis=0, keepdims=True))
        shifted = jnp.concatenate([stats[:, :, 16:], stats[:, :, :16]], axis=2)
        sc[...] = w / jnp.sum(w * shifted, axis=0, keepdims=True)

        def add(j, acc):
            one = sc[j]
            scale = jnp.concatenate([one[:, 32 * s : 32 * s + 1] for s in range(SL)], axis=0)
            return acc + scale * br[k, j].astype(F32)

        latent = lax.fori_loop(0, EP, add, jnp.zeros((SL * HP, LAT), F32)).astype(BF)
        values = jnp.zeros((SL * HP, VD), F32)
        for h in range(HP):
            values = jnp.where(head_of == h, dot(latent, vw[h]), values)
        values = values.astype(BF)
        cs[k] = values
        cr[k, dp] = values
        loop(1, DP, lambda i: c_copy(k, i).start())

    loads[6].wait()
    merge(0)
    merge(1)
    loads[7].wait()

    lanes = HP * VC
    pick = jnp.where(
        iota((VD, lanes), 0) == dp * VC + (iota((VD, lanes), 1) & (VC - 1)), 1.0, 0.0
    ).astype(BF)
    vc_bits = VC.bit_length() - 1
    keep = (iota((DP * SL * HP, lanes), 0) & (HP - 1)) == (iota((DP * SL * HP, lanes), 1) >> vc_bits)
    used = []
    for k in range(2):
        loop(1, DP, lambda i: c_wait(k, i))
        picked = dot(cr[k].reshape(DP * SL * HP, VD), pick)
        picked = jnp.where(keep, picked, 0.0)
        used.append(jnp.sum(picked.reshape(DP * SL, HP, lanes), axis=1))
    used = dot(place, jnp.concatenate(used, axis=0).astype(BF)).astype(BF)

    own_rows = pl.ds(pl.multiple_of(core * HALF, 16), HALF)
    other_rows = pl.ds(pl.multiple_of((1 - core) * HALF, 16), HALF)
    sibling = z * 2 + (1 - core)

    def reduce_scatter(product, pc, pr, xs, xr, zs, zr, s_c, r_c, s_x, r_x, s_z, r_z):
        def c_copy(j):
            return remote(pc.at[j, other_rows], pr.at[j], s_c.at[j], r_c.at[j], sibling, ep)

        def x_copy(j):
            return remote(xs.at[j], xr.at[ep], s_x.at[j], r_x.at[ep], dp, j)

        def z_copy(i):
            t = (z + i) % NZ
            return remote(zs.at[t], zr.at[z], s_z.at[t], r_z.at[z], t * 2 + core, ep)

        def pair(i):
            return (ep // 2 + 1 + i) % (EP // 2)

        def first(i):
            jp = pair(i)
            part = product(pl.ds(pl.multiple_of(jp * 2 * BW, 128), 2 * BW))
            pc[2 * jp] = part[:, :BW].astype(BF)
            pc[2 * jp + 1] = part[:, BW:].astype(BF)
            c_copy(2 * jp).start()
            c_copy(2 * jp + 1).start()

        loop(0, EP // 2, first)

        def second(i):
            for t in range(2):
                j = 2 * pair(i) + t
                c_copy(j).wait_recv()
                part = (pc[j, own_rows].astype(F32) + pr[j].astype(F32)).astype(BF)
                xs[j] = part

                @pl.when(j != ep)
                def _():
                    x_copy(j).start()

        loop(0, EP // 2, second)
        xr[ep] = xs[ep]

        def x_wait(i):
            j = to_ep(i)
            remote(xs.at[j], xr.at[j], s_x.at[j], r_x.at[j], dp, j).wait_recv()

        loop(1, EP, x_wait)
        total = lax.fori_loop(
            0, EP, lambda j, acc: acc + xr[j].astype(F32), jnp.zeros((HALF, BW), F32)
        )
        zs[...] = total.reshape(NZ, 8, BW)
        zr[z] = zs[z]
        loop(1, NZ, lambda i: z_copy(i).start())

        def z_wait(i):
            t = (z + i) % NZ
            remote(zs.at[t], zr.at[t], s_z.at[t], r_z.at[t], t * 2 + core, ep).wait_recv()

        loop(1, NZ, z_wait)
        result = jnp.sum(zr[...], axis=0)

        def finish():
            loop(0, EP, lambda j: c_copy(j).wait_send())
            loop(1, EP, lambda i: x_copy(to_ep(i)).wait_send())
            loop(1, NZ, lambda i: z_copy(i).wait_send())

        return result, finish

    attn, finish_one = reduce_scatter(
        lambda cols: dot(used, ow[:, cols]),
        pc, pr, xs, xr, zs, zr, s1c, r1c, s1x, r1x, s1z, r1z,
    )
    own_resid = jnp.concatenate([resid[0].astype(F32), resid[1].astype(F32)], axis=0)
    hidden = own_resid + attn

    gs[:, :BW] = hidden * gain[...]
    gs[:, BW:] = jnp.broadcast_to(
        jnp.sum(hidden * hidden, axis=1, keepdims=True), (8, gs.shape[1] - BW)
    )
    gr[z] = gs[...]

    def gz_copy(i):
        t = (z + i) % NZ
        return remote(gs, gr.at[z], sgz.at[t], rgz.at[z], t * 2 + core, ep)

    def gz_wait(i):
        t = (z + i) % NZ
        remote(gs, gr.at[t], sgz.at[t], rgz.at[t], t * 2 + core, ep).wait_recv()

    def gx_copy(i):
        e = to_ep(i)
        block = hb.at[ep, own_rows]
        return remote(block, block, sgx.at[e], rgx.at[ep], dp, e)

    def gx_wait(e):
        block = hb.at[e, own_rows]
        remote(block, block, sgx.at[e], rgx.at[e], dp, e).wait_recv()

    def gc_copy(e):
        block = hb.at[e, own_rows]
        return remote(block, block, sgc.at[e], rgc.at[e], sibling, ep)

    def gc_wait(e):
        block = hb.at[e, other_rows]
        remote(block, block, sgc.at[e], rgc.at[e], sibling, ep).wait_recv()

    loop(1, NZ, lambda i: gz_copy(i).start())
    loop(1, NZ, gz_wait)
    wide = gr[...].reshape(HALF, gs.shape[1])
    hi = wide.astype(BF).astype(F32)
    mid = (wide - hi).astype(BF).astype(F32)
    lo = wide - hi - mid
    lane = iota(wide.shape, 1)
    hb[ep, own_rows] = jnp.where(
        lane <= BW, hi, jnp.where(lane == BW + 1, mid, lo)
    ).astype(BF)
    loop(1, EP, lambda i: gx_copy(i).start())
    gc_copy(ep).start()
    loads[8].wait()
    loads[9].wait()

    def project(e, acc):
        proj, squares = acc
        block = hb[e]
        w = gu[pl.ds(pl.multiple_of(e * BW, 16), BW), :]
        tail = block[:, 384:].astype(F32)
        return proj + dot(block[:, :BW], w), squares + tail

    def step(i, acc):
        e = (ep + EP - i) % EP
        gx_wait(e)
        gc_copy(e).start()
        before = (ep + EP - i + 1) % EP
        gc_wait(before)
        return project(before, acc)

    acc = (jnp.zeros((ROWS, 256), F32), jnp.zeros((ROWS, 128), F32))
    acc = lax.fori_loop(1, EP, step, acc)
    last = (ep + 1) % EP
    gc_wait(last)
    proj, squares = project(last, acc)
    off = BW - 384
    square = squares[:, off : off + 1] + squares[:, off + 1 : off + 2] + squares[:, off + 2 : off + 3]
    scale = lax.rsqrt(square / float(BW * EP) + NORM_EPS)
    g = proj[:, :128] * scale
    u = proj[:, 128:] * scale
    act = (g / (1.0 + jnp.exp(-g)) * u).astype(BF)
    loads[10].wait()
    route = rw[:, 0:1]
    routed, finish_two = reduce_scatter(
        lambda cols: dot(act, dn[:, cols]) * route,
        pc2, pr2, xs2, xr2, zs2, zr2, s2c, r2c, s2x, r2x, s2z, r2z,
    )
    mixed = (hidden + routed).astype(out.dtype)
    out[0] = mixed[0:4]
    out[1] = mixed[4:8]

    loop(1, DP, lambda k: a1(k).wait_send())
    loop(1, EP, lambda k: a2(k).wait_send())
    for k in range(2):
        loop(1, EP, lambda i: b_copy(k, i).wait_send())
        loop(1, EP, lambda i: t_copy(k, i).wait_send())
        loop(1, DP, lambda i: c_copy(k, i).wait_send())
    finish_one()
    loop(1, NZ, lambda i: gz_copy(i).wait_send())
    loop(1, EP, lambda i: gx_copy(i).wait_send())
    loop(0, EP, lambda e: gc_copy(e).wait_send())
    finish_two()


def body(
    DP, EP,
    latent_cache, lengths, queries, fresh_latent, leaving, target, value_weight, output_weight,
    residual_stream, norm_gain, expert_ids, gate_codes, gate_weight, up_weight, down_weight,
):
    SL, T, LW = latent_cache.shape
    H = queries.shape[2]
    HP, _, VD = value_weight.shape
    D = norm_gain.shape[0]
    BW = D // EP
    NZ = DP // 2
    ROWS = DP * 8
    HALF = ROWS // 2
    PIECE = 768 // EP
    dp = lax.axis_index("dp")
    ep = lax.axis_index("ep")
    cache = jnp.swapaxes(latent_cache, 1, 2)
    q = jnp.swapaxes(queries, 2, 3)
    gain = lax.dynamic_slice_in_dim(norm_gain, ep * BW, BW, 0).astype(F32).reshape(1, BW)
    resid = lax.dynamic_slice(residual_stream, (0, dp * SL, ep * BW), (2, SL, BW))
    ow = output_weight.reshape(HP * output_weight.shape[1], D)
    smem = pl.BlockSpec(memory_space=pltpu.SMEM)
    vmem = pl.BlockSpec(memory_space=pltpu.VMEM)
    anyw = pl.BlockSpec(memory_space=pl.ANY)
    V = pltpu.VMEM
    sems = lambda *n: pltpu.SemaphoreType.DMA(n)
    rs_bufs = [
        V((EP, ROWS, BW), BF), V((EP, HALF, BW), BF), V((EP, HALF, BW), BF), V((EP, HALF, BW), BF),
        V((NZ, 8, BW), F32), V((NZ, 8, BW), F32),
    ]
    rs_sems = [sems(EP), sems(EP), sems(EP), sems(EP), sems(NZ), sems(NZ)]
    scratch = [
        V((SL, LW, H), BF), V((SL, LW, H), BF), V((SL, LW, T), BF), V(value_weight.shape, BF), V(ow.shape, BF),
        V((D, 256), BF), V((128, D), BF),
        V((768, 128), BF), V((DP, PIECE, 128), BF), V((PIECE, 128), BF), V((768, 128), BF), V((16, LW), BF),
        V((2, EP, SL * HP, LAT), BF), V((2, EP, HP, 128), F32), V((2, EP, SL * HP, LAT), BF),
        V((2, EP, HP, 128), F32), V((EP, HP, 128), F32), V((SL * HP, LAT), BF),
        V((2, SL * HP, VD), BF), V((2, DP, SL * HP, VD), BF),
        *rs_bufs, *rs_bufs,
        V((8, 512), F32), V((NZ, 8, 512), F32), V((EP, ROWS, 512), BF), V((ROWS, 128), F32),
        sems(11), sems(DP), sems(DP), sems(EP), sems(EP), sems(2, EP), sems(2, EP), sems(2, EP), sems(2, EP),
        sems(2, DP), sems(2, DP),
        *rs_sems, *rs_sems,
        sems(NZ), sems(NZ), sems(EP), sems(EP), sems(EP), sems(EP),
    ]
    return pl.pallas_call(
        functools.partial(kernel, DP, EP),
        out_shape=jax.ShapeDtypeStruct((2, SL, BW), BF),
        in_specs=[smem] * 3 + [vmem] * 5 + [anyw] * 7,
        out_specs=vmem,
        scratch_shapes=scratch,
        compiler_params=pltpu.CompilerParams(
            collective_id=0, has_side_effects=True, vmem_limit_bytes=56 * 2**20
        ),
        name="decode",
    )(
        lengths, leaving, target, fresh_latent,
        jnp.swapaxes(expert_ids, 1, 2), jnp.swapaxes(gate_codes, 1, 2), gain, resid,
        cache, q, value_weight, ow, gate_weight[0], up_weight[0], down_weight[0],
    )


def solution(mesh):
    placed = (
        P("dp", "ep", None), P(), P(None, "dp", None, None), P(None, "dp", None), P(), P(),
        P("ep", None, None), P("ep", "dp", None), P(), P(), P(), P(),
        P("ep", None, "dp"), P("ep", None, "dp"), P("ep", "dp", None),
    )
    return jax.shard_map(
        functools.partial(body, mesh.shape["dp"], mesh.shape["ep"]),
        mesh=mesh, in_specs=placed, out_specs=P(None, "dp", "ep"), check_vma=False,
    )
```

```python
import functools

import jax
import jax.numpy as jnp
from jax import lax
from jax.experimental import pallas as pl
from jax.experimental.pallas import tpu as pltpu
from jax.sharding import PartitionSpec as P

MESH = pl.DeviceIdType.MESH
SCORE_SCALE = 192.0 ** (-0.5)
ROUTE_SCALE = 2.5
NORM_EPS = 1e-06
MASKED = -1e30
LAT = 512
BF = jnp.bfloat16
F32 = jnp.float32


def iota(shape, dim):
    return lax.broadcasted_iota(jnp.int32, shape, dim)


def dot(a, b, ca=1, cb=0):
    return lax.dot_general(a, b, (((ca,), (cb,)), ((), ())), preferred_element_type=F32)


def loop(lo, hi, fn):
    lax.fori_loop(lo, hi, lambda i, c: (fn(i), c)[1], 0)


def kernel(
    DP, EP,
    lengths, leaving, target, fresh, ids, codes, gain, resid,
    cache_h, q_h, vw_h, ow_h, gate_h, up_h, down_h,
    out,
    q1v, q2v, cv, vw, gu, rv,
    owr, dnr, us, ur, az, ar,
    a1s, a1r, a2s, a2r, fk,
    bs, bt, br, btr, sc, lat,
    cs, cr,
    es1, er1, es2, er2,
    gs, gr, hb, rw,
    ld, sa1, ra1, sa2, ra2, sb, rb, st, rt, scs, rcs,
    sow, row_, sdn, rdn, su, ru, sact, ract,
    s1, r1, s2, r2,
    sgz, rgz, sgx, rgx, sgc, rgc,
):
    NZ = DP // 2
    SL = 4
    HP = vw.shape[0]
    VD = vw.shape[2]
    VC = VD // DP
    ROWS = DP * 8
    HALF = ROWS // 2
    BW = owr.shape[2] - 64
    WIN = owr.shape[2]
    LW = cv.shape[1]
    T = cv.shape[2]
    HEADS = q1v.shape[2]
    PIECE = a2s.shape[0]
    dp = lax.axis_index("dp")
    ep = lax.axis_index("ep")
    z = dp // 2
    core = dp % 2

    def to_dp(k):
        return (dp + k) % DP

    def to_ep(k):
        return (ep + k) % EP

    def remote(src, dst, s, r, d, e):
        return pltpu.make_async_remote_copy(
            src_ref=src, dst_ref=dst, send_sem=s, recv_sem=r, device_id=(d, e), device_id_type=MESH
        )

    def local(src, dst, k):
        return pltpu.make_async_copy(src, dst, ld.at[k])

    def window(e):
        start = (e // 2) * 2 * BW + (e % 2) * (2 * BW - WIN)
        return pl.ds(pl.multiple_of(start, 128), WIN)

    pair_cols = pl.ds(pl.multiple_of((ep // 2) * 2 * BW, 128), 2 * BW)
    group_rows = pl.ds(pl.multiple_of((dp // 4) * 16, 16), 16)
    loads = [local(q_h.at[1], q2v, 0), local(q_h.at[0], q1v, 1)]
    loads += [local(cache_h.at[s], cv.at[s], 2 + s) for s in range(SL)]
    loads += [
        local(vw_h, vw, 6),
        local(resid.at[:, group_rows, pair_cols], rv, 7),
        local(gate_h, gu.at[:, pl.ds(0, 128)], 8),
        local(up_h, gu.at[:, pl.ds(128, 128)], 9),
        local(ow_h.at[:, window(ep)], owr.at[ep], 10),
        local(down_h.at[:, window(ep)], dnr.at[ep], 11),
    ]
    for c in loads:
        c.start()

    barrier = pltpu.get_barrier_semaphore()
    loop(1, DP, lambda k: pl.semaphore_signal(barrier, inc=1, device_id=(to_dp(k), ep), device_id_type=MESH))
    loop(1, EP, lambda k: pl.semaphore_signal(barrier, inc=1, device_id=(dp, to_ep(k)), device_id_type=MESH))

    lv = leaving[dp]
    f0 = fresh[0].astype(F32)
    f1 = fresh[1].astype(F32)
    frow = jnp.sum(jnp.where(iota(f1.shape, 0) == lv, f1, 0.0), axis=0, keepdims=True)
    frow = jnp.concatenate([frow, jnp.zeros((1, 640 - LW), F32)], axis=1)
    fpieces = [frow[:, 128 * i : 128 * (i + 1)] for i in range(5)]
    loads[0].wait()
    a1s[0:LW, 0:HEADS] = q2v[lv]
    a1s[LW : LW + 16] = jnp.concatenate(fpieces + [jnp.zeros((11, 128), F32)], axis=0).astype(BF)
    a1s[LW + 16 :] = jnp.zeros((a1s.shape[0] - LW - 16, 128), BF)
    mine = pl.ds(pl.multiple_of(ep * PIECE, 16), PIECE)
    a1r[dp] = a1s[mine]
    pl.semaphore_wait(barrier, DP + EP - 2)

    def a1(k):
        d = to_dp(k)
        return remote(a1s.at[mine], a1r.at[dp], sa1.at[d], ra1.at[dp], d, ep)

    loop(1, DP, lambda k: a1(k).start())

    def ow_copy(i):
        e = to_ep(i)
        return remote(ow_h.at[:, window(e)], owr.at[ep], sow.at[e], row_.at[ep], dp, e)

    def dn_copy(i):
        e = to_ep(i)
        return remote(down_h.at[:, window(e)], dnr.at[ep], sdn.at[e], rdn.at[ep], dp, e)

    def ow_wait(i):
        e = to_ep(i)
        remote(ow_h.at[:, window(e)], owr.at[e], sow.at[e], row_.at[e], dp, e).wait_recv()

    def dn_wait(i):
        e = to_ep(i)
        remote(down_h.at[:, window(e)], dnr.at[e], sdn.at[e], rdn.at[e], dp, e).wait_recv()

    loop(1, EP, lambda i: ow_copy(i).start())
    loop(1, EP // 2, lambda i: dn_copy(i).start())

    def attend(q, s, live_fresh):
        kt = cv[s]
        score = dot(q, kt, 0, 0) * SCORE_SCALE
        pos = ep * T + iota(score.shape, 1)
        live = pos < lengths[dp * SL + s]
        fkeys = fk[...]
        fscore = dot(q, fkeys, 0, 1) * SCORE_SCALE
        score = jnp.where(live, score, MASKED)
        fscore = jnp.where(live_fresh, fscore, MASKED)
        peak = jnp.maximum(
            jnp.max(score, axis=1, keepdims=True), jnp.max(fscore, axis=1, keepdims=True)
        )
        w = jnp.where(live, jnp.exp(score - peak), 0.0)
        fw = jnp.where(live_fresh, jnp.exp(fscore - peak), 0.0)
        total = jnp.sum(w, axis=1, keepdims=True) + jnp.sum(fw, axis=1, keepdims=True)
        v = dot(w.astype(BF), kt[:LAT], 1, 1) + dot(fw.astype(BF), fkeys[:, :LAT])
        return peak, total, v

    group = iota((HEADS, 128), 1) >> 4

    def attend_step(k, query_of, live_of):
        stat = jnp.zeros((HEADS, 128), F32)
        for p in range(SL // 2):
            both = []
            for s in (2 * p, 2 * p + 1):
                peak, total, v = attend(query_of(s), s, live_of(s))
                stat = jnp.where(group == 2 * s, peak, jnp.where(group == 2 * s + 1, total, stat))
                both.append(v.reshape(EP, HP, LAT))
            bs[k, :, 16 * p : 16 * p + 16, :] = jnp.concatenate(both, axis=1).astype(BF)
        bt[k] = stat.reshape(EP, HP, 128)
        br[k, ep] = bs[k, ep]
        btr[k, ep] = bt[k, ep]

    def b_copy(k, i):
        e = to_ep(i)
        return remote(bs.at[k, e], br.at[k, ep], sb.at[k, e], rb.at[k, ep], dp, e)

    def t_copy(k, i):
        e = to_ep(i)
        return remote(bt.at[k, e], btr.at[k, ep], st.at[k, e], rt.at[k, ep], dp, e)

    def b_wait(k, i):
        e = to_ep(i)
        remote(bs.at[k, e], br.at[k, e], sb.at[k, e], rb.at[k, e], dp, e).wait_recv()
        remote(bt.at[k, e], btr.at[k, e], st.at[k, e], rt.at[k, e], dp, e).wait_recv()

    def b_start(k):
        def go(i):
            t_copy(k, i).start()
            b_copy(k, i).start()

        loop(1, EP, go)

    fcol = iota((1, 16), 1)
    at_zero = ep == 0
    fk[...] = jnp.concatenate([f0, f1, jnp.zeros((8, LW), F32)], axis=0).astype(BF)
    loads[1].wait()
    for s in range(SL):
        loads[2 + s].wait()
    attend_step(0, lambda s: q1v[s], lambda s: (fcol == s) & at_zero)

    def a1_wait(k):
        d = to_dp(k)
        remote(a1s.at[mine], a1r.at[d], sa1.at[d], ra1.at[d], d, ep).wait_recv()

    loop(1, DP, a1_wait)
    piece = a1r[target[dp]]
    a2s[...] = piece
    a2r[mine] = piece

    def a2(k):
        e = to_ep(k)
        return remote(a2s, a2r.at[mine], sa2.at[e], ra2.at[ep], dp, e)

    def a2_wait(k):
        e = to_ep(k)
        rows = pl.ds(pl.multiple_of(e * PIECE, 16), PIECE)
        remote(a2s, a2r.at[rows], sa2.at[e], ra2.at[e], dp, e).wait_recv()

    loop(1, EP, lambda k: a2(k).start())
    b_start(0)

    row = iota((ROWS, 2 * SL * DP), 0)
    col = iota((ROWS, 2 * SL * DP), 1)
    half_bits = HALF.bit_length() - 1
    r_core = row >> half_bits
    r_z = (row >> 3) & (NZ - 1)
    r_step = (row >> 2) & 1
    slot = (r_z * 2 + r_core) * SL + (row & 3)
    held = slot
    for r in range(DP):
        t = target[r]
        held = jnp.where(slot == t * SL + leaving[t], r * SL + leaving[r], held)
    place = (r_step * (SL * DP) + jnp.where(r_step == 1, held, slot)) == col
    code = codes[...].astype(F32)
    share = code / jnp.sum(code, axis=1, keepdims=True) * ROUTE_SCALE
    weight = jnp.sum(jnp.where(ids[...] == ep, share, 0.0), axis=1)
    weight = jnp.concatenate([weight[0:1], weight[1:2]], axis=1)
    own_place = (r_step * (SL * DP) + slot) == col
    rw[...] = jnp.broadcast_to(
        jnp.sum(jnp.where(own_place, weight, 0.0), axis=1, keepdims=True), (ROWS, 128)
    )
    place = jnp.where(place, 1.0, 0.0).astype(BF)
    odd_block = ep % 2 == 1
    lines = 2 * BW // 128
    seven = jnp.zeros((lines, 128), F32)
    for i in range(EP // 2):
        seven = jnp.where(ep // 2 == i, gain[lines * i : lines * (i + 1)], seven)
    seven = jnp.concatenate([seven[i : i + 1] for i in range(lines)], axis=1)
    own_gain = jnp.where(odd_block, seven[:, BW:], seven[:, :BW])
    loads[7].wait()
    wide = rv[...].astype(F32)
    own_resid = jnp.zeros((8, 2 * BW), F32)
    for i in range(4):
        rows = jnp.concatenate([wide[0, 4 * i : 4 * i + 4], wide[1, 4 * i : 4 * i + 4]], axis=0)
        own_resid = jnp.where(dp % 4 == i, rows, own_resid)
    own_resid = jnp.where(odd_block, own_resid[:, BW:], own_resid[:, :BW])

    loop(1, EP, a2_wait)
    moved_f = a2r[LW : LW + 16].astype(F32)
    moved_f = jnp.concatenate([moved_f[i : i + 1] for i in range(5)], axis=1)[:, :LW]
    fk[...] = jnp.concatenate([f0, f1, moved_f, jnp.zeros((7, LW), F32)], axis=0).astype(BF)
    moved_q = a2r[0:LW, 0:HEADS]
    attend_step(
        1,
        lambda s: jnp.where(lv == s, moved_q, q2v[s]),
        lambda s: ((fcol == s) | (fcol == jnp.where(lv == s, 8, 4 + s))) & at_zero,
    )
    b_start(1)

    head_of = iota((SL * HP, VD), 0) & (HP - 1)

    def c_copy(k, i):
        d = to_dp(i)
        return remote(cs.at[k], cr.at[k, dp], scs.at[k, d], rcs.at[k, dp], d, ep)

    def c_wait(k, i):
        d = to_dp(i)
        remote(cs.at[k], cr.at[k, d], scs.at[k, d], rcs.at[k, d], d, ep).wait_recv()

    def merge(k):
        loop(1, EP, lambda i: b_wait(k, i))
        stats = btr[k]
        w = jnp.exp(stats - jnp.max(stats, axis=0, keepdims=True))
        shifted = jnp.concatenate([stats[:, :, 16:], stats[:, :, :16]], axis=2)
        sc[...] = w / jnp.sum(w * shifted, axis=0, keepdims=True)

        def add(j, acc):
            one = sc[j]
            scale = jnp.concatenate([one[:, 32 * s : 32 * s + 1] for s in range(SL)], axis=0)
            return acc + scale * br[k, j].astype(F32)

        latent = lax.fori_loop(0, EP, add, jnp.zeros((SL * HP, LAT), F32)).astype(BF)
        values = jnp.zeros((SL * HP, VD), F32)
        for h in range(HP):
            values = jnp.where(head_of == h, dot(latent, vw[h]), values)
        values = values.astype(BF)
        cs[k] = values
        cr[k, dp] = values
        loop(1, DP, lambda i: c_copy(k, i).start())

    loads[6].wait()
    merge(0)
    merge(1)
    loop(EP // 2, EP, lambda i: dn_copy(i).start())

    lanes = HP * VC
    pick = jnp.where(
        iota((VD, lanes), 0) == dp * VC + (iota((VD, lanes), 1) & (VC - 1)), 1.0, 0.0
    ).astype(BF)
    vc_bits = VC.bit_length() - 1
    keep = (iota((DP * SL * HP, lanes), 0) & (HP - 1)) == (iota((DP * SL * HP, lanes), 1) >> vc_bits)
    used = []
    for k in range(2):
        loop(1, DP, lambda i: c_wait(k, i))
        picked = dot(cr[k].reshape(DP * SL * HP, VD), pick)
        picked = jnp.where(keep, picked, 0.0)
        used.append(jnp.sum(picked.reshape(DP * SL, HP, lanes), axis=1))
    used = dot(place, jnp.concatenate(used, axis=0).astype(BF)).astype(BF)

    def u_copy(i):
        e = to_ep(i)
        return remote(us, ur.at[ep], su.at[e], ru.at[ep], dp, e)

    def u_wait(i):
        e = to_ep(i)
        remote(us, ur.at[e], su.at[e], ru.at[e], dp, e).wait_recv()

    us[...] = used
    ur[ep] = used
    loop(1, EP, lambda i: u_copy(i).start())

    own_rows = pl.ds(pl.multiple_of(core * HALF, 16), HALF)
    other_rows = pl.ds(pl.multiple_of((1 - core) * HALF, 16), HALF)
    sibling = z * 2 + (1 - core)
    my_block = core * NZ + z
    odd = ep % 2 == 1
    HB = BW // 2

    def own_columns(part):
        return jnp.where(odd, part[:, WIN - BW :], part[:, :BW])

    def sum_over_dp(part, es, er, s_e, r_e):
        part = part.reshape(DP, 8, BW)
        es[...] = jnp.concatenate([part[:, :, :HB], part[:, :, HB:]], axis=1).astype(BF)
        er[my_block] = es[my_block]

        def e_copy(i):
            d = to_dp(i)
            b = (d % 2) * NZ + d // 2
            return remote(es.at[b], er.at[my_block], s_e.at[b], r_e.at[my_block], d, ep)

        def e_wait(i):
            d = to_dp(i)
            b = (d % 2) * NZ + d // 2
            remote(es.at[b], er.at[b], s_e.at[b], r_e.at[b], d, ep).wait_recv()

        loop(1, DP, lambda i: e_copy(i).start())
        loop(1, DP, e_wait)
        total = jnp.sum(er[...].astype(F32), axis=0)
        return jnp.concatenate([total[:8], total[8:]], axis=1), lambda: loop(
            1, DP, lambda i: e_copy(i).wait_send()
        )

    loads[10].wait()
    loop(1, EP, ow_wait)
    loop(1, EP, u_wait)
    every = jnp.concatenate([ur[e] for e in range(EP)], axis=1)
    part = own_columns(dot(every, owr[...].reshape(EP * owr.shape[1], WIN)))
    attn, finish_one = sum_over_dp(part, es1, er1, s1, r1)
    hidden = own_resid + attn

    scaled = hidden * own_gain
    square = jnp.sum(hidden * hidden, axis=1, keepdims=True)
    hi = square.astype(BF).astype(F32)
    mid = (square - hi).astype(BF).astype(F32)
    lane = iota((8, 256 - HB), 1)
    extra = jnp.where(lane == 0, hi, jnp.where(lane == 1, mid, square - hi - mid))
    gs[...] = jnp.concatenate(
        [
            jnp.concatenate([scaled[:, :HB], extra], axis=1),
            jnp.concatenate([scaled[:, HB:], jnp.zeros_like(extra)], axis=1),
        ],
        axis=0,
    ).astype(BF)
    gr[z] = gs[...]

    def gz_copy(i):
        t = (z + i) % NZ
        return remote(gs, gr.at[z], sgz.at[t], rgz.at[z], t * 2 + core, ep)

    def gz_wait(i):
        t = (z + i) % NZ
        remote(gs, gr.at[t], sgz.at[t], rgz.at[t], t * 2 + core, ep).wait_recv()

    def gx_copy(i):
        e = to_ep(i)
        block = hb.at[ep, own_rows]
        return remote(block, block, sgx.at[e], rgx.at[ep], dp, e)

    def gx_wait(e):
        block = hb.at[e, own_rows]
        remote(block, block, sgx.at[e], rgx.at[e], dp, e).wait_recv()

    def gc_copy(e):
        block = hb.at[e, own_rows]
        return remote(block, block, sgc.at[e], rgc.at[e], sibling, ep)

    def gc_wait(e):
        block = hb.at[e, other_rows]
        remote(block, block, sgc.at[e], rgc.at[e], sibling, ep).wait_recv()

    loop(1, NZ, lambda i: gz_copy(i).start())
    loop(1, NZ, gz_wait)
    wide = gr[...].astype(F32)
    top, low = wide[:, :8], wide[:, 8:]
    wide = jnp.concatenate([top[:, :, :HB], low[:, :, :HB], top[:, :, HB:], low[:, :, HB:]], axis=2)
    hb[ep, own_rows] = wide.reshape(HALF, 512).astype(BF)
    loop(1, EP, lambda i: gx_copy(i).start())
    gc_copy(ep).start()
    loads[8].wait()
    loads[9].wait()

    def project(e, acc):
        proj, squares = acc
        block = hb[e]
        w = gu[pl.ds(pl.multiple_of(e * BW, 16), BW), :]
        tail = block[:, 384:].astype(F32)
        return proj + dot(block[:, :BW], w), squares + tail

    def step(i, acc):
        e = (ep + EP - i) % EP
        gx_wait(e)
        gc_copy(e).start()
        before = (ep + EP - i + 1) % EP
        gc_wait(before)
        return project(before, acc)

    acc = (jnp.zeros((ROWS, 256), F32), jnp.zeros((ROWS, 128), F32))
    acc = lax.fori_loop(1, EP, step, acc)
    last = (ep + 1) % EP
    gc_wait(last)
    proj, squares = project(last, acc)
    off = BW - 384
    square = squares[:, off : off + 1] + squares[:, off + 1 : off + 2] + squares[:, off + 2 : off + 3]
    scale = lax.rsqrt(square / float(BW * EP) + NORM_EPS)
    g = proj[:, :128] * scale
    u = proj[:, 128:] * scale
    act = (g / (1.0 + jnp.exp(-g)) * u * rw[:, 0:1]).astype(BF)
    az[...] = act
    ar[ep] = act

    def act_copy(i):
        e = to_ep(i)
        return remote(az, ar.at[ep], sact.at[e], ract.at[ep], dp, e)

    def act_wait(i):
        e = to_ep(i)
        remote(az, ar.at[e], sact.at[e], ract.at[e], dp, e).wait_recv()

    loop(1, EP, lambda i: act_copy(i).start())
    loads[11].wait()
    loop(1, EP, dn_wait)
    loop(1, EP, act_wait)
    every = jnp.concatenate([ar[e] for e in range(EP)], axis=1)
    part = own_columns(dot(every, dnr[...].reshape(EP * 128, WIN)))
    routed, finish_two = sum_over_dp(part, es2, er2, s2, r2)
    mixed = (hidden + routed).astype(out.dtype)
    out[0] = mixed[0:4]
    out[1] = mixed[4:8]

    loop(1, DP, lambda k: a1(k).wait_send())
    loop(1, EP, lambda k: a2(k).wait_send())
    for k in range(2):
        loop(1, EP, lambda i: b_copy(k, i).wait_send())
        loop(1, EP, lambda i: t_copy(k, i).wait_send())
        loop(1, DP, lambda i: c_copy(k, i).wait_send())
    finish_one()
    loop(1, NZ, lambda i: gz_copy(i).wait_send())
    loop(1, EP, lambda i: gx_copy(i).wait_send())
    loop(0, EP, lambda e: gc_copy(e).wait_send())
    finish_two()
    loop(1, EP, lambda i: ow_copy(i).wait_send())
    loop(1, EP, lambda i: dn_copy(i).wait_send())
    loop(1, EP, lambda i: u_copy(i).wait_send())
    loop(1, EP, lambda i: act_copy(i).wait_send())


def body(
    DP, EP,
    latent_cache, lengths, queries, fresh_latent, leaving, target, value_weight, output_weight,
    residual_stream, norm_gain, expert_ids, gate_codes, gate_weight, up_weight, down_weight,
):
    SL, T, LW = latent_cache.shape
    H = queries.shape[2]
    HP, _, VD = value_weight.shape
    D = norm_gain.shape[0]
    BW = D // EP
    NZ = DP // 2
    ROWS = DP * 8
    HALF = ROWS // 2
    PIECE = 768 // EP
    cache = jnp.swapaxes(latent_cache, 1, 2)
    q = jnp.swapaxes(queries, 2, 3)
    gain = norm_gain.astype(F32).reshape(D // 128, 128)
    ow = output_weight.reshape(HP * output_weight.shape[1], D)
    smem = pl.BlockSpec(memory_space=pltpu.SMEM)
    vmem = pl.BlockSpec(memory_space=pltpu.VMEM)
    anyw = pl.BlockSpec(memory_space=pl.ANY)
    V = pltpu.VMEM
    sems = lambda *n: pltpu.SemaphoreType.DMA(n)
    scratch = [
        V((SL, LW, H), BF), V((SL, LW, H), BF), V((SL, LW, T), BF), V(value_weight.shape, BF),
        V((D, 256), BF), V((2, 16, 2 * BW), BF),
        V((EP, ow.shape[0], BW + 64), BF), V((EP, 128, BW + 64), BF),
        V((ROWS, ow.shape[0]), BF), V((EP, ROWS, ow.shape[0]), BF), V((ROWS, 128), BF), V((EP, ROWS, 128), BF),
        V((768, 128), BF), V((DP, PIECE, 128), BF), V((PIECE, 128), BF), V((768, 128), BF), V((16, LW), BF),
        V((2, EP, SL * HP, LAT), BF), V((2, EP, HP, 128), F32), V((2, EP, SL * HP, LAT), BF),
        V((2, EP, HP, 128), F32), V((EP, HP, 128), F32), V((SL * HP, LAT), BF),
        V((2, SL * HP, VD), BF), V((2, DP, SL * HP, VD), BF),
        *[V((DP, 16, BW // 2), BF)] * 4,
        V((16, 256), BF), V((NZ, 16, 256), BF), V((EP, ROWS, 512), BF), V((ROWS, 128), F32),
        sems(12), sems(DP), sems(DP), sems(EP), sems(EP), sems(2, EP), sems(2, EP), sems(2, EP), sems(2, EP),
        sems(2, DP), sems(2, DP),
        *[sems(EP)] * 8, *[sems(DP)] * 4,
        sems(NZ), sems(NZ), sems(EP), sems(EP), sems(EP), sems(EP),
    ]
    return pl.pallas_call(
        functools.partial(kernel, DP, EP),
        out_shape=jax.ShapeDtypeStruct((2, SL, BW), BF),
        in_specs=[smem] * 3 + [vmem] * 4 + [anyw] * 8,
        out_specs=vmem,
        scratch_shapes=scratch,
        compiler_params=pltpu.CompilerParams(
            collective_id=0, has_side_effects=True, vmem_limit_bytes=56 * 2**20
        ),
        name="decode",
    )(
        lengths, leaving, target, fresh_latent,
        jnp.swapaxes(expert_ids, 1, 2), jnp.swapaxes(gate_codes, 1, 2), gain, residual_stream,
        cache, q, value_weight, ow, gate_weight[0], up_weight[0], down_weight[0],
    )


def solution(mesh):
    placed = (
        P("dp", "ep", None), P(), P(None, "dp", None, None), P(None, "dp", None), P(), P(),
        P("ep", None, None), P("ep", "dp", None), P(), P(), P(), P(),
        P("ep", None, "dp"), P("ep", None, "dp"), P("ep", "dp", None),
    )
    return jax.shard_map(
        functools.partial(body, mesh.shape["dp"], mesh.shape["ep"]),
        mesh=mesh, in_specs=placed, out_specs=P(None, "dp", "ep"), check_vma=False,
    )
```

```python
import functools

import jax
import jax.numpy as jnp
from jax import lax
from jax.experimental import pallas as pl
from jax.experimental.pallas import tpu as pltpu
from jax.sharding import PartitionSpec as P

MESH = pl.DeviceIdType.MESH
SCORE_SCALE = 192.0 ** (-0.5)
ROUTE_SCALE = 2.5
NORM_EPS = 1e-06
MASKED = -1e30
LAT = 512
BF = jnp.bfloat16
F32 = jnp.float32


def iota(shape, dim):
    return lax.broadcasted_iota(jnp.int32, shape, dim)


def dot(a, b, ca=1, cb=0):
    return lax.dot_general(a, b, (((ca,), (cb,)), ((), ())), preferred_element_type=F32)


def loop(lo, hi, fn):
    lax.fori_loop(lo, hi, lambda i, c: (fn(i), c)[1], 0)


class Exchange:
    def __init__(self, moves, lo, hi, copy, arrive):
        self.lo, self.hi, self.copy, self.arrive = lo, hi, copy, arrive
        moves.append(self)

    def start(self):
        loop(self.lo, self.hi, lambda i: self.copy(i).start())

    def wait(self):
        loop(self.lo, self.hi, lambda i: self.arrive(i).wait_recv())

    def finish(self):
        loop(self.lo, self.hi, lambda i: self.copy(i).wait_send())


def kernel(
    DP, EP,
    lengths, leaving, target, fresh, ids, codes, gain, resid,
    cache_h, q_h, vw_h, ow_h, gate_h, up_h, down_h,
    out,
    q1v, q2v, cv, vw, gu, rv,
    owr, us, ur, dn,
    a1s, a1r, a2s, a2r, fk,
    bs, bt, br, btr, sc, lat,
    cs, cr,
    es1, er1, pc, pr, xs, xr, zs, zr,
    gs, gr, hb, rw,
    ld, sa1, ra1, sa1c, ra1c, sa2, ra2, sb, rb, st, rt, scs, rcs,
    sow, row_, su, ru, s1, r1,
    s2c, r2c, s2x, r2x, s2z, r2z,
    sgz, rgz, sgx, rgx, sgc, rgc,
):
    NZ = DP // 2
    SL = 4
    HP = vw.shape[0]
    VD = vw.shape[2]
    VC = VD // DP
    ROWS = DP * 8
    HALF = ROWS // 2
    BW = owr.shape[2] - 64
    WIN = owr.shape[2]
    LW = cv.shape[1]
    T = cv.shape[2]
    HEADS = q1v.shape[2]
    PIECE = a2s.shape[0]
    dp = lax.axis_index("dp")
    ep = lax.axis_index("ep")
    z = dp // 2
    core = dp % 2
    sibling = z * 2 + (1 - core)

    def to_dp(k):
        return (dp + k) % DP

    def to_ep(k):
        return (ep + k) % EP

    def remote(src, dst, s, r, d, e):
        return pltpu.make_async_remote_copy(
            src_ref=src, dst_ref=dst, send_sem=s, recv_sem=r, device_id=(d, e), device_id_type=MESH
        )

    moves = []

    def spread_dp(lo, hi, src, dst, s, r):
        def copy(i):
            d = to_dp(i)
            return remote(src(d), dst(dp), s.at[d], r.at[dp], d, ep)

        def arrive(i):
            d = to_dp(DP - i)
            return remote(src(d), dst(d), s.at[d], r.at[d], d, ep)

        return Exchange(moves, lo, hi, copy, arrive)

    def spread_ep(lo, hi, src, dst, s, r):
        def copy(i):
            e = to_ep(i)
            return remote(src(e), dst(ep), s.at[e], r.at[ep], dp, e)

        def arrive(i):
            e = to_ep(EP - i)
            return remote(src(e), dst(e), s.at[e], r.at[e], dp, e)

        return Exchange(moves, lo, hi, copy, arrive)

    def local(src, dst, k):
        return pltpu.make_async_copy(src, dst, ld.at[k])

    def window(e):
        start = (e // 2) * 2 * BW + (e % 2) * (2 * BW - WIN)
        return pl.ds(pl.multiple_of(start, 128), WIN)

    pair_cols = pl.ds(pl.multiple_of((ep // 2) * 2 * BW, 128), 2 * BW)
    group_rows = pl.ds(pl.multiple_of((dp // 4) * 16, 16), 16)
    loads = [local(q_h.at[1], q2v, 0), local(q_h.at[0], q1v, 1)]
    loads += [local(cache_h.at[s], cv.at[s], 2 + s) for s in range(SL)]
    loads += [
        local(vw_h, vw, 6),
        local(resid.at[:, group_rows, pair_cols], rv, 7),
        local(gate_h, gu.at[:, pl.ds(0, 128)], 8),
        local(up_h, gu.at[:, pl.ds(128, 128)], 9),
        local(ow_h.at[:, window(ep)], owr.at[ep], 10),
        local(down_h, dn, 11),
    ]
    loads[0].start()

    barrier = pltpu.get_barrier_semaphore()
    loop(1, DP, lambda k: pl.semaphore_signal(barrier, inc=1, device_id=(to_dp(k), ep), device_id_type=MESH))
    loop(1, EP, lambda k: pl.semaphore_signal(barrier, inc=1, device_id=(dp, to_ep(k)), device_id_type=MESH))

    lv = leaving[dp]
    f0 = fresh[0].astype(F32)
    f1 = fresh[1].astype(F32)
    frow = jnp.sum(jnp.where(iota(f1.shape, 0) == lv, f1, 0.0), axis=0, keepdims=True)
    frow = jnp.concatenate([frow, jnp.zeros((1, 640 - LW), F32)], axis=1)
    fpieces = [frow[:, 128 * i : 128 * (i + 1)] for i in range(5)]
    loads[0].wait()
    a1s[0:LW, 0:HEADS] = q2v[lv]
    a1s[LW : LW + 16] = jnp.concatenate(fpieces + [jnp.zeros((11, 128), F32)], axis=0).astype(BF)
    a1s[LW + 16 :] = jnp.zeros((a1s.shape[0] - LW - 16, 128), BF)
    mine = pl.ds(pl.multiple_of(ep * PIECE, 16), PIECE)
    a1r[core, z] = a1s[mine]
    pl.semaphore_wait(barrier, DP + EP - 2)

    def spread_z(src, dst, s, r):
        def copy(i):
            t = (z + i) % NZ
            return remote(src(t), dst(z), s.at[t], r.at[z], t * 2 + core, ep)

        def arrive(i):
            t = (z + NZ - i) % NZ
            return remote(src(t), dst(t), s.at[t], r.at[t], t * 2 + core, ep)

        return Exchange(moves, 1, NZ, copy, arrive)

    a1 = spread_z(lambda t: a1s.at[mine], lambda t: a1r.at[core, t], sa1, ra1)
    a1.start()
    for c in loads[1:]:
        c.start()

    def ow_from(e):
        return ow_h.at[:, window(e)]

    ow_x = spread_ep(1, EP // 2, ow_from, lambda e: owr.at[e], sow, row_)
    ow_y = spread_ep(EP // 2, EP, ow_from, lambda e: owr.at[e], sow, row_)
    ow_x.start()

    def attend(q, s, live_fresh, fkeys):
        kt = cv[s]
        score = dot(q, kt, 0, 0) * SCORE_SCALE
        pos = ep * T + iota(score.shape, 1)
        live = pos < lengths[dp * SL + s]
        fscore = dot(q, fkeys, 0, 1) * SCORE_SCALE
        score = jnp.where(live, score, MASKED)
        fscore = jnp.where(live_fresh, fscore, MASKED)
        peak = jnp.maximum(
            jnp.max(score, axis=1, keepdims=True), jnp.max(fscore, axis=1, keepdims=True)
        )
        w = jnp.where(live, jnp.exp(score - peak), 0.0)
        fw = jnp.where(live_fresh, jnp.exp(fscore - peak), 0.0)
        total = jnp.sum(w, axis=1, keepdims=True) + jnp.sum(fw, axis=1, keepdims=True)
        v = dot(w.astype(BF), kt[:LAT], 1, 1) + dot(fw.astype(BF), fkeys[:, :LAT])
        return peak, total, v

    group = iota((HEADS, 128), 1) >> 4

    def attend_step(k, query_of, live_of):
        stat = jnp.zeros((HEADS, 128), F32)
        for p in range(SL // 2):
            both = []
            for s in (2 * p, 2 * p + 1):
                peak, total, v = attend(query_of(s), s, live_of(s), fk[...])
                stat = jnp.where(group == 2 * s, peak, jnp.where(group == 2 * s + 1, total, stat))
                both.append(v.reshape(EP, HP, LAT))
            bs[k, :, 16 * p : 16 * p + 16, :] = jnp.concatenate(both, axis=1).astype(BF)
        bt[k] = stat.reshape(EP, HP, 128)

    def keep_own(k):
        br[k, ep] = bs[k, ep]
        btr[k, ep] = bt[k, ep]

    def partial_exchange(k):
        return (
            spread_ep(1, EP, lambda e: bt.at[k, e], lambda e: btr.at[k, e], st.at[k], rt.at[k]),
            spread_ep(1, EP, lambda e: bs.at[k, e], lambda e: br.at[k, e], sb.at[k], rb.at[k]),
        )

    b_x = [partial_exchange(0), partial_exchange(1)]

    fcol = iota((1, 16), 1)
    at_zero = ep == 0
    fk[...] = jnp.concatenate([f0, f1, jnp.zeros((8, LW), F32)], axis=0).astype(BF)
    loads[1].wait()
    for s in range(SL):
        loads[2 + s].wait()
    attend_step(0, lambda s: q1v[s], lambda s: (fcol == s) & at_zero)
    keep_own(0)

    a1.wait()
    a1c = Exchange(
        moves, 0, 1,
        lambda i: remote(a1r.at[core], a1r.at[core], sa1c, ra1c, sibling, ep),
        lambda i: remote(a1r.at[1 - core], a1r.at[1 - core], sa1c, ra1c, sibling, ep),
    )
    a1c.start()
    a1c.wait()
    other = target[dp]
    piece = a1r[other & 1, other >> 1]
    a2s[...] = piece
    a2r[mine] = piece

    def piece_rows(e):
        return a2r.at[pl.ds(pl.multiple_of(e * PIECE, 16), PIECE)]

    a2 = spread_ep(1, EP, lambda e: a2s, piece_rows, sa2, ra2)
    a2.start()
    for x in b_x[0]:
        x.start()

    row = iota((ROWS, 2 * SL * DP), 0)
    col = iota((ROWS, 2 * SL * DP), 1)
    half_bits = HALF.bit_length() - 1
    r_core = row >> half_bits
    r_z = (row >> 3) & (NZ - 1)
    r_step = (row >> 2) & 1
    slot = (r_z * 2 + r_core) * SL + (row & 3)
    held = slot
    for r in range(DP):
        t = target[r]
        held = jnp.where(slot == t * SL + leaving[t], r * SL + leaving[r], held)
    place = (r_step * (SL * DP) + jnp.where(r_step == 1, held, slot)) == col
    code = codes[...].astype(F32)
    share = code / jnp.sum(code, axis=1, keepdims=True) * ROUTE_SCALE
    weight = jnp.sum(jnp.where(ids[...] == ep, share, 0.0), axis=1)
    weight = jnp.concatenate([weight[0:1], weight[1:2]], axis=1)
    own_place = (r_step * (SL * DP) + slot) == col
    rw[...] = jnp.broadcast_to(
        jnp.sum(jnp.where(own_place, weight, 0.0), axis=1, keepdims=True), (ROWS, 128)
    )
    place = jnp.where(place, 1.0, 0.0).astype(BF)
    odd_block = ep % 2 == 1
    lines = 2 * BW // 128
    seven = jnp.zeros((lines, 128), F32)
    for i in range(EP // 2):
        seven = jnp.where(ep // 2 == i, gain[lines * i : lines * (i + 1)], seven)
    seven = jnp.concatenate([seven[i : i + 1] for i in range(lines)], axis=1)
    own_gain = jnp.where(odd_block, seven[:, BW:], seven[:, :BW])
    loads[7].wait()
    wide = rv[...].astype(F32)
    own_resid = jnp.zeros((8, 2 * BW), F32)
    for i in range(4):
        rows = jnp.concatenate([wide[0, 4 * i : 4 * i + 4], wide[1, 4 * i : 4 * i + 4]], axis=0)
        own_resid = jnp.where(dp % 4 == i, rows, own_resid)
    own_resid = jnp.where(odd_block, own_resid[:, BW:], own_resid[:, :BW])

    attend_step(1, lambda s: q2v[s], lambda s: ((fcol == s) | (fcol == 4 + s)) & at_zero)
    a2.wait()
    moved_f = a2r[LW : LW + 16].astype(F32)
    moved_f = jnp.concatenate([moved_f[i : i + 1] for i in range(5)], axis=1)[:, :LW]
    fkeys = jnp.concatenate([f0, f1, moved_f, jnp.zeros((7, LW), F32)], axis=0).astype(BF)
    peak, total, v = attend(
        a2r[0:LW, 0:HEADS], lv, ((fcol == lv) | (fcol == 8)) & at_zero, fkeys
    )
    v = v.reshape(EP, HP, LAT)
    twice = jnp.concatenate([v, v], axis=1)
    upper = iota(twice.shape, 1) >> 3
    for p in range(SL // 2):
        rows = bs[1, :, 16 * p : 16 * p + 16, :].astype(F32)
        bs[1, :, 16 * p : 16 * p + 16, :] = jnp.where(upper + 2 * p == lv, twice, rows).astype(BF)
    stat = bt[1].reshape(HEADS, 128)
    stat = jnp.where(group == 2 * lv, peak, jnp.where(group == 2 * lv + 1, total, stat))
    bt[1] = stat.reshape(EP, HP, 128)
    keep_own(1)
    for x in b_x[1]:
        x.start()

    head_of = iota((SL * HP, VD), 0) & (HP - 1)

    def value_exchange(k):
        return spread_dp(
            1, DP, lambda d: cs.at[k], lambda d: cr.at[k, d], scs.at[k], rcs.at[k]
        )

    c_x = [value_exchange(0), value_exchange(1)]

    def merge(k):
        for x in b_x[k]:
            x.wait()
        if k == 1:
            ow_y.start()
        stats = btr[k]
        w = jnp.exp(stats - jnp.max(stats, axis=0, keepdims=True))
        shifted = jnp.concatenate([stats[:, :, 16:], stats[:, :, :16]], axis=2)
        sc[...] = w / jnp.sum(w * shifted, axis=0, keepdims=True)

        def add(j, acc):
            one = sc[j]
            scale = jnp.concatenate([one[:, 32 * s : 32 * s + 1] for s in range(SL)], axis=0)
            return acc + scale * br[k, j].astype(F32)

        latent = lax.fori_loop(0, EP, add, jnp.zeros((SL * HP, LAT), F32)).astype(BF)
        values = jnp.zeros((SL * HP, VD), F32)
        for h in range(HP):
            values = jnp.where(head_of == h, dot(latent, vw[h]), values)
        values = values.astype(BF)
        cs[k] = values
        cr[k, dp] = values
        c_x[k].start()

    loads[6].wait()
    merge(0)
    merge(1)

    lanes = HP * VC
    pick = jnp.where(
        iota((VD, lanes), 0) == dp * VC + (iota((VD, lanes), 1) & (VC - 1)), 1.0, 0.0
    ).astype(BF)
    vc_bits = VC.bit_length() - 1
    keep = (iota((DP * SL * HP, lanes), 0) & (HP - 1)) == (iota((DP * SL * HP, lanes), 1) >> vc_bits)
    used = []
    for k in range(2):
        c_x[k].wait()
        picked = dot(cr[k].reshape(DP * SL * HP, VD), pick)
        picked = jnp.where(keep, picked, 0.0)
        used.append(jnp.sum(picked.reshape(DP * SL, HP, lanes), axis=1))
    used = dot(place, jnp.concatenate(used, axis=0).astype(BF)).astype(BF)

    u_x = spread_ep(1, EP, lambda e: us, lambda e: ur.at[e], su, ru)
    us[...] = used
    ur[ep] = used
    u_x.start()

    own_rows = pl.ds(pl.multiple_of(core * HALF, 16), HALF)
    other_rows = pl.ds(pl.multiple_of((1 - core) * HALF, 16), HALF)
    my_block = core * NZ + z
    odd = ep % 2 == 1
    HB = BW // 2

    def own_columns(part):
        return jnp.where(odd, part[:, WIN - BW :], part[:, :BW])

    def sum_over_dp(part, es, er, s_e, r_e):
        part = part.reshape(DP, 8, BW)
        es[...] = jnp.concatenate([part[:, :, :HB], part[:, :, HB:]], axis=1).astype(BF)
        er[my_block] = es[my_block]

        def e_copy(i):
            d = to_dp(i)
            b = (d % 2) * NZ + d // 2
            return remote(es.at[b], er.at[my_block], s_e.at[b], r_e.at[my_block], d, ep)

        def e_arrive(i):
            d = to_dp(i)
            b = (d % 2) * NZ + d // 2
            return remote(es.at[b], er.at[b], s_e.at[b], r_e.at[b], d, ep)

        x = Exchange(moves, 1, DP, e_copy, e_arrive)
        x.start()
        x.wait()
        total = jnp.sum(er[...].astype(F32), axis=0)
        return jnp.concatenate([total[:8], total[8:]], axis=1)

    loads[10].wait()
    ow_x.wait()
    ow_y.wait()
    u_x.wait()
    every = jnp.concatenate([ur[e] for e in range(EP)], axis=1)
    part = own_columns(dot(every, owr[...].reshape(EP * owr.shape[1], WIN)))
    attn = sum_over_dp(part, es1, er1, s1, r1)
    hidden = own_resid + attn

    scaled = hidden * own_gain
    square = jnp.sum(hidden * hidden, axis=1, keepdims=True)
    hi = square.astype(BF).astype(F32)
    mid = (square - hi).astype(BF).astype(F32)
    lane = iota((8, 256 - HB), 1)
    extra = jnp.where(lane == 0, hi, jnp.where(lane == 1, mid, square - hi - mid))
    gs[...] = jnp.concatenate(
        [
            jnp.concatenate([scaled[:, :HB], extra], axis=1),
            jnp.concatenate([scaled[:, HB:], jnp.zeros_like(extra)], axis=1),
        ],
        axis=0,
    ).astype(BF)
    gr[z] = gs[...]

    gz_x = spread_z(lambda t: gs, lambda t: gr.at[t], sgz, rgz)

    def gx_copy(i):
        e = to_ep(i)
        block = hb.at[ep, own_rows]
        return remote(block, block, sgx.at[e], rgx.at[ep], dp, e)

    def gx_wait(e):
        block = hb.at[e, own_rows]
        remote(block, block, sgx.at[e], rgx.at[e], dp, e).wait_recv()

    def gc_copy(e):
        block = hb.at[e, own_rows]
        return remote(block, block, sgc.at[e], rgc.at[e], sibling, ep)

    def gc_wait(e):
        block = hb.at[e, other_rows]
        remote(block, block, sgc.at[e], rgc.at[e], sibling, ep).wait_recv()

    gz_x.start()
    gz_x.wait()
    wide = gr[...].astype(F32)
    top, low = wide[:, :8], wide[:, 8:]
    wide = jnp.concatenate([top[:, :, :HB], low[:, :, :HB], top[:, :, HB:], low[:, :, HB:]], axis=2)
    hb[ep, own_rows] = wide.reshape(HALF, 512).astype(BF)
    loop(1, EP, lambda i: gx_copy(i).start())
    gc_copy(ep).start()
    loads[8].wait()
    loads[9].wait()

    def project(e, acc):
        proj, squares = acc
        block = hb[e]
        w = gu[pl.ds(pl.multiple_of(e * BW, 16), BW), :]
        tail = block[:, 384:].astype(F32)
        return proj + dot(block[:, :BW], w), squares + tail

    def step(i, acc):
        e = (ep + EP - i) % EP
        gx_wait(e)
        gc_copy(e).start()
        before = (ep + EP - i + 1) % EP
        gc_wait(before)
        return project(before, acc)

    acc = (jnp.zeros((ROWS, 256), F32), jnp.zeros((ROWS, 128), F32))
    acc = lax.fori_loop(1, EP, step, acc)
    last = (ep + 1) % EP
    gc_wait(last)
    proj, squares = project(last, acc)
    off = BW - 384
    square = squares[:, off : off + 1] + squares[:, off + 1 : off + 2] + squares[:, off + 2 : off + 3]
    scale = lax.rsqrt(square / float(BW * EP) + NORM_EPS)
    g = proj[:, :128] * scale
    u = proj[:, 128:] * scale
    act = (g / (1.0 + jnp.exp(-g)) * u * rw[:, 0:1]).astype(BF)
    loads[11].wait()

    def c_copy(j):
        return remote(pc.at[j, other_rows], pr.at[j], s2c.at[j], r2c.at[j], sibling, ep)

    def x_copy(j):
        return remote(xs.at[j], xr.at[ep], s2x.at[j], r2x.at[ep], dp, j)

    def pair(i):
        return (ep // 2 + 1 + i) % (EP // 2)

    def first(i):
        jp = pair(i)
        part = dot(act, dn[:, pl.ds(pl.multiple_of(jp * 2 * BW, 128), 2 * BW)])
        pc[2 * jp] = part[:, :BW].astype(BF)
        pc[2 * jp + 1] = part[:, BW:].astype(BF)
        c_copy(2 * jp).start()
        c_copy(2 * jp + 1).start()

    def second(i):
        for t in range(2):
            j = 2 * pair(i) + t
            c_copy(j).wait_recv()
            xs[j] = (pc[j, own_rows].astype(F32) + pr[j].astype(F32)).astype(BF)

            @pl.when(j != ep)
            def _():
                x_copy(j).start()

    def both(i):
        first(i)
        second(i - 1)

    first(0)
    loop(1, EP // 2, both)
    second(EP // 2 - 1)

    def x_sum(i, acc):
        j = to_ep(EP - i)
        remote(xs.at[j], xr.at[j], s2x.at[j], r2x.at[j], dp, j).wait_recv()
        return acc + xr[j].astype(F32)

    total = lax.fori_loop(1, EP, x_sum, xs[ep].astype(F32))
    total = total.reshape(NZ, 8, BW)
    zs[...] = jnp.concatenate([total[:, :, :HB], total[:, :, HB:]], axis=1).astype(BF)
    zr[z] = zs[z]
    z_x = spread_z(lambda t: zs.at[t], lambda t: zr.at[t], s2z, r2z)
    z_x.start()
    z_x.wait()
    total = jnp.sum(zr[...].astype(F32), axis=0)
    routed = jnp.concatenate([total[:8], total[8:]], axis=1)
    mixed = (hidden + routed).astype(out.dtype)
    out[0] = mixed[0:4]
    out[1] = mixed[4:8]

    for x in moves:
        x.finish()
    loop(1, EP, lambda i: gx_copy(i).wait_send())
    loop(0, EP, lambda e: gc_copy(e).wait_send())
    loop(0, EP, lambda j: c_copy(j).wait_send())
    loop(1, EP, lambda i: x_copy(to_ep(i)).wait_send())


def body(
    DP, EP,
    latent_cache, lengths, queries, fresh_latent, leaving, target, value_weight, output_weight,
    residual_stream, norm_gain, expert_ids, gate_codes, gate_weight, up_weight, down_weight,
):
    SL, T, LW = latent_cache.shape
    H = queries.shape[2]
    HP, _, VD = value_weight.shape
    D = norm_gain.shape[0]
    BW = D // EP
    NZ = DP // 2
    ROWS = DP * 8
    HALF = ROWS // 2
    PIECE = 768 // EP
    cache = jnp.swapaxes(latent_cache, 1, 2)
    q = jnp.swapaxes(queries, 2, 3)
    gain = norm_gain.astype(F32).reshape(D // 128, 128)
    ow = output_weight.reshape(HP * output_weight.shape[1], D)
    smem = pl.BlockSpec(memory_space=pltpu.SMEM)
    vmem = pl.BlockSpec(memory_space=pltpu.VMEM)
    anyw = pl.BlockSpec(memory_space=pl.ANY)
    V = pltpu.VMEM
    sems = lambda *n: pltpu.SemaphoreType.DMA(n)
    scratch = [
        V((SL, LW, H), BF), V((SL, LW, H), BF), V((SL, LW, T), BF), V(value_weight.shape, BF),
        V((D, 256), BF), V((2, 16, 2 * BW), BF),
        V((EP, ow.shape[0], BW + 64), BF),
        V((ROWS, ow.shape[0]), BF), V((EP, ROWS, ow.shape[0]), BF), V((128, D), BF),
        V((768, 128), BF), V((2, NZ, PIECE, 128), BF), V((PIECE, 128), BF), V((768, 128), BF), V((16, LW), BF),
        V((2, EP, SL * HP, LAT), BF), V((2, EP, HP, 128), F32), V((2, EP, SL * HP, LAT), BF),
        V((2, EP, HP, 128), F32), V((EP, HP, 128), F32), V((SL * HP, LAT), BF),
        V((2, SL * HP, VD), BF), V((2, DP, SL * HP, VD), BF),
        *[V((DP, 16, BW // 2), BF)] * 2,
        V((EP, ROWS, BW), BF), *[V((EP, HALF, BW), BF)] * 3, *[V((NZ, 16, BW // 2), BF)] * 2,
        V((16, 256), BF), V((NZ, 16, 256), BF), V((EP, ROWS, 512), BF), V((ROWS, 128), F32),
        sems(12), sems(NZ), sems(NZ), pltpu.SemaphoreType.DMA, pltpu.SemaphoreType.DMA, sems(EP), sems(EP), sems(2, EP), sems(2, EP), sems(2, EP), sems(2, EP),
        sems(2, DP), sems(2, DP),
        *[sems(EP)] * 4, *[sems(DP)] * 2, *[sems(EP)] * 4, *[sems(NZ)] * 2,
        sems(NZ), sems(NZ), sems(EP), sems(EP), sems(EP), sems(EP),
    ]
    return pl.pallas_call(
        functools.partial(kernel, DP, EP),
        out_shape=jax.ShapeDtypeStruct((2, SL, BW), BF),
        in_specs=[smem] * 3 + [vmem] * 4 + [anyw] * 8,
        out_specs=vmem,
        scratch_shapes=scratch,
        compiler_params=pltpu.CompilerParams(
            collective_id=0, has_side_effects=True, vmem_limit_bytes=56 * 2**20
        ),
        name="decode",
    )(
        lengths, leaving, target, fresh_latent,
        jnp.swapaxes(expert_ids, 1, 2), jnp.swapaxes(gate_codes, 1, 2), gain, residual_stream,
        cache, q, value_weight, ow, gate_weight[0], up_weight[0], down_weight[0],
    )


def solution(mesh):
    placed = (
        P("dp", "ep", None), P(), P(None, "dp", None, None), P(None, "dp", None), P(), P(),
        P("ep", None, None), P("ep", "dp", None), P(), P(), P(), P(),
        P("ep", None, "dp"), P("ep", None, "dp"), P("ep", "dp", None),
    )
    return jax.shard_map(
        functools.partial(body, mesh.shape["dp"], mesh.shape["ep"]),
        mesh=mesh, in_specs=placed, out_specs=P(None, "dp", "ep"), check_vma=False,
    )
```

```python
import functools

import jax
import jax.numpy as jnp
from jax import lax
from jax.experimental import pallas as pl
from jax.experimental.pallas import tpu as pltpu
from jax.sharding import PartitionSpec as P

MESH = pl.DeviceIdType.MESH
SCORE_SCALE = 192.0 ** (-0.5)
ROUTE_SCALE = 2.5
NORM_EPS = 1e-06
MASKED = -1e30
LAT = 512
BF = jnp.bfloat16
F32 = jnp.float32


def iota(shape, dim):
    return lax.broadcasted_iota(jnp.int32, shape, dim)


def dot(a, b, ca=1, cb=0):
    return lax.dot_general(a, b, (((ca,), (cb,)), ((), ())), preferred_element_type=F32)


def loop(lo, hi, fn):
    lax.fori_loop(lo, hi, lambda i, c: (fn(i), c)[1], 0)


class Exchange:
    def __init__(self, moves, lo, hi, copy, arrive):
        self.lo, self.hi, self.copy, self.arrive = lo, hi, copy, arrive
        moves.append(self)

    def start(self):
        loop(self.lo, self.hi, lambda i: self.copy(i).start())

    def wait(self):
        loop(self.lo, self.hi, lambda i: self.arrive(i).wait_recv())

    def finish(self):
        loop(self.lo, self.hi, lambda i: self.copy(i).wait_send())


def kernel(
    DP, EP,
    lengths, leaving, target, fresh, ids, codes, gain, resid,
    cache_h, q_h, vw_h, ow_h, gate_h, up_h, down_h,
    out,
    q1v, q2v, cv, vw, gu, rv,
    owr, owp, vals, dn,
    a1s, a1r, a2s, a2r, fk,
    bs, bt, br, btr, sc, lat,
    cs, cr,
    es1, er1, pc, pr, xs, xr, zs, zr,
    gs, hb, rw,
    ld, sa1, ra1, sa1c, ra1c, sa2, ra2, sb, rb, st, rt, scs, rcs,
    sow, row_, s1, r1,
    s2c, r2c, s2x, r2x, s2z, r2z,
    sgz, rgz, sgx, rgx, sgc, rgc,
):
    NZ = DP // 2
    SL = 4
    HP = vw.shape[0]
    VD = vw.shape[2]
    VC = VD // DP
    ROWS = DP * 8
    HALF = ROWS // 2
    BW = owr.shape[2] - 64
    WIN = owr.shape[2]
    HB = BW // 2
    LW = cv.shape[1]
    T = cv.shape[2]
    HEADS = q1v.shape[2]
    PIECE = a2s.shape[0]
    dp = lax.axis_index("dp")
    ep = lax.axis_index("ep")
    z = dp // 2
    core = dp % 2
    sibling = z * 2 + (1 - core)

    def to_dp(k):
        return (dp + k) % DP

    def to_ep(k):
        return (ep + k) % EP

    def remote(src, dst, s, r, d, e):
        return pltpu.make_async_remote_copy(
            src_ref=src, dst_ref=dst, send_sem=s, recv_sem=r, device_id=(d, e), device_id_type=MESH
        )

    moves = []

    def spread_dp(lo, hi, src, dst, s, r):
        def copy(i):
            d = to_dp(i)
            return remote(src(d), dst(dp), s.at[d], r.at[dp], d, ep)

        def arrive(i):
            d = to_dp(DP - i)
            return remote(src(d), dst(d), s.at[d], r.at[d], d, ep)

        return Exchange(moves, lo, hi, copy, arrive)

    def spread_ep(lo, hi, src, dst, s, r):
        def copy(i):
            e = to_ep(i)
            return remote(src(e), dst(ep), s.at[e], r.at[ep], dp, e)

        def arrive(i):
            e = to_ep(EP - i)
            return remote(src(e), dst(e), s.at[e], r.at[e], dp, e)

        return Exchange(moves, lo, hi, copy, arrive)

    def local(src, dst, k):
        return pltpu.make_async_copy(src, dst, ld.at[k])

    def window(e):
        start = (e // 2) * 2 * BW + (e % 2) * (2 * BW - WIN)
        return pl.ds(pl.multiple_of(start, 128), WIN)

    row_group = ep // 2
    col_half = ep % 2
    first_core, first_z = (2 * row_group) // NZ, (2 * row_group) % NZ
    pair_cols = pl.ds(pl.multiple_of((dp // 2) * 2 * BW, 128), 2 * BW)
    group_rows = pl.ds(pl.multiple_of(first_z * 8, 16), 16)
    loads = [local(q_h.at[1], q2v, 0), local(q_h.at[0], q1v, 1)]
    loads += [local(cache_h.at[s], cv.at[s], 2 + s) for s in range(SL)]
    loads += [
        local(vw_h, vw, 6),
        local(resid.at[:, group_rows, pair_cols], rv, 7),
        local(gate_h, gu.at[:, pl.ds(0, 128)], 8),
        local(up_h, gu.at[:, pl.ds(128, 128)], 9),
        local(ow_h.at[:, window(dp)], owr.at[dp], 10),
        local(down_h, dn, 11),
    ]
    loads[0].start()

    barrier = pltpu.get_barrier_semaphore()
    loop(1, DP, lambda k: pl.semaphore_signal(barrier, inc=1, device_id=(to_dp(k), ep), device_id_type=MESH))
    loop(1, EP, lambda k: pl.semaphore_signal(barrier, inc=1, device_id=(dp, to_ep(k)), device_id_type=MESH))

    lv = leaving[dp]
    f0 = fresh[0].astype(F32)
    f1 = fresh[1].astype(F32)
    frow = jnp.sum(jnp.where(iota(f1.shape, 0) == lv, f1, 0.0), axis=0, keepdims=True)
    frow = jnp.concatenate([frow, jnp.zeros((1, 640 - LW), F32)], axis=1)
    fpieces = [frow[:, 128 * i : 128 * (i + 1)] for i in range(5)]
    loads[0].wait()
    a1s[0:LW, 0:HEADS] = q2v[lv]
    a1s[LW : LW + 16] = jnp.concatenate(fpieces + [jnp.zeros((11, 128), F32)], axis=0).astype(BF)
    a1s[LW + 16 :] = jnp.zeros((a1s.shape[0] - LW - 16, 128), BF)
    mine = pl.ds(pl.multiple_of(ep * PIECE, 16), PIECE)
    a1r[core, z] = a1s[mine]
    pl.semaphore_wait(barrier, DP + EP - 2)

    def spread_z(src, dst, s, r):
        def copy(i):
            t = (z + i) % NZ
            return remote(src(t), dst(z), s.at[t], r.at[z], t * 2 + core, ep)

        def arrive(i):
            t = (z + NZ - i) % NZ
            return remote(src(t), dst(t), s.at[t], r.at[t], t * 2 + core, ep)

        return Exchange(moves, 1, NZ, copy, arrive)

    a1 = spread_z(lambda t: a1s.at[mine], lambda t: a1r.at[core, t], sa1, ra1)
    a1.start()
    for c in loads[1:]:
        c.start()

    ow_x = spread_dp(1, DP, lambda d: ow_h.at[:, window(d)], lambda d: owr.at[d], sow, row_)

    def attend(q, s, live_fresh, fkeys):
        kt = cv[s]
        score = dot(q, kt, 0, 0) * SCORE_SCALE
        pos = ep * T + iota(score.shape, 1)
        live = pos < lengths[dp * SL + s]
        fscore = dot(q, fkeys, 0, 1) * SCORE_SCALE
        score = jnp.where(live, score, MASKED)
        fscore = jnp.where(live_fresh, fscore, MASKED)
        peak = jnp.maximum(
            jnp.max(score, axis=1, keepdims=True), jnp.max(fscore, axis=1, keepdims=True)
        )
        w = jnp.where(live, jnp.exp(score - peak), 0.0)
        fw = jnp.where(live_fresh, jnp.exp(fscore - peak), 0.0)
        total = jnp.sum(w, axis=1, keepdims=True) + jnp.sum(fw, axis=1, keepdims=True)
        v = dot(w.astype(BF), kt[:LAT], 1, 1) + dot(fw.astype(BF), fkeys[:, :LAT])
        return peak, total, v

    group = iota((HEADS, 128), 1) >> 4

    def attend_step(k, query_of, live_of):
        stat = jnp.zeros((HEADS, 128), F32)
        for p in range(SL // 2):
            both = []
            for s in (2 * p, 2 * p + 1):
                peak, total, v = attend(query_of(s), s, live_of(s), fk[...])
                stat = jnp.where(group == 2 * s, peak, jnp.where(group == 2 * s + 1, total, stat))
                both.append(v.reshape(EP, HP, LAT))
            bs[k, :, 16 * p : 16 * p + 16, :] = jnp.concatenate(both, axis=1).astype(BF)
        bt[k] = stat.reshape(EP, HP, 128)

    def keep_own(k):
        br[k, ep] = bs[k, ep]
        btr[k, ep] = bt[k, ep]

    def partial_exchange(k):
        return (
            spread_ep(1, EP, lambda e: bt.at[k, e], lambda e: btr.at[k, e], st.at[k], rt.at[k]),
            spread_ep(1, EP, lambda e: bs.at[k, e], lambda e: br.at[k, e], sb.at[k], rb.at[k]),
        )

    b_x = [partial_exchange(0), partial_exchange(1)]

    fcol = iota((1, 16), 1)
    at_zero = ep == 0
    fk[...] = jnp.concatenate([f0, f1, jnp.zeros((8, LW), F32)], axis=0).astype(BF)
    loads[1].wait()
    for s in range(SL):
        loads[2 + s].wait()
    attend_step(0, lambda s: q1v[s], lambda s: (fcol == s) & at_zero)
    keep_own(0)

    a1.wait()
    a1c = Exchange(
        moves, 0, 1,
        lambda i: remote(a1r.at[core], a1r.at[core], sa1c, ra1c, sibling, ep),
        lambda i: remote(a1r.at[1 - core], a1r.at[1 - core], sa1c, ra1c, sibling, ep),
    )
    a1c.start()
    a1c.wait()
    ow_x.start()
    other = target[dp]
    piece = a1r[other & 1, other >> 1]
    a2s[...] = piece
    a2r[mine] = piece

    def piece_rows(e):
        return a2r.at[pl.ds(pl.multiple_of(e * PIECE, 16), PIECE)]

    a2 = spread_ep(1, EP, lambda e: a2s, piece_rows, sa2, ra2)
    a2.start()
    for x in b_x[0]:
        x.start()

    row = iota((ROWS, 2 * SL * DP), 0)
    col = iota((ROWS, 2 * SL * DP), 1)
    half_bits = HALF.bit_length() - 1
    r_core = row >> half_bits
    r_z = (row >> 3) & (NZ - 1)
    r_step = (row >> 2) & 1
    slot = (r_z * 2 + r_core) * SL + (row & 3)
    held = slot
    for r in range(DP):
        t = target[r]
        held = jnp.where(slot == t * SL + leaving[t], r * SL + leaving[r], held)
    held = jnp.where(r_step == 1, held, slot)
    place = ((held >> 2) * 8 + r_step * 4 + (held & 3)) == col
    code = codes[...].astype(F32)
    share = code / jnp.sum(code, axis=1, keepdims=True) * ROUTE_SCALE
    weight = jnp.sum(jnp.where(ids[...] == ep, share, 0.0), axis=1)
    weight = jnp.concatenate([weight[0:1], weight[1:2]], axis=1)
    own_place = (r_step * (SL * DP) + slot) == col
    rw[...] = jnp.broadcast_to(
        jnp.sum(jnp.where(own_place, weight, 0.0), axis=1, keepdims=True), (ROWS, 128)
    )
    place = jnp.where(place, 1.0, 0.0).astype(BF)
    lines = 2 * BW // 128
    seven = jnp.zeros((lines, 128), F32)
    mixed_gain = jnp.zeros((lines, 128), F32)
    for i in range(EP // 2):
        seven = jnp.where(dp // 2 == i, gain[lines * i : lines * (i + 1)], seven)
        mixed_gain = jnp.where(ep // 2 == i, gain[lines * i : lines * (i + 1)], mixed_gain)
    seven = jnp.concatenate([seven[i : i + 1] for i in range(lines)], axis=1)
    mixed_gain = jnp.concatenate([mixed_gain[i : i + 1] for i in range(lines)], axis=1)
    mixed_gain = jnp.where(ep % 2 == 1, mixed_gain[:, BW:], mixed_gain[:, :BW])

    def quarter(wide):
        out = wide[:, :HB]
        for i in range(1, 4):
            out = jnp.where((dp % 2) * 2 + col_half == i, wide[:, HB * i : HB * (i + 1)], out)
        return out

    own_gain = quarter(seven)
    loads[7].wait()
    wide = rv[...].astype(F32)
    own_resid = [
        jnp.where(first_core == 0, wide[k, 8 * t : 8 * t + 4], wide[k, 8 * t + 4 : 8 * t + 8])
        for t in range(2)
        for k in range(2)
    ]
    own_resid = quarter(jnp.concatenate(own_resid, axis=0))

    attend_step(1, lambda s: q2v[s], lambda s: ((fcol == s) | (fcol == 4 + s)) & at_zero)
    a2.wait()
    moved_f = a2r[LW : LW + 16].astype(F32)
    moved_f = jnp.concatenate([moved_f[i : i + 1] for i in range(5)], axis=1)[:, :LW]
    fkeys = jnp.concatenate([f0, f1, moved_f, jnp.zeros((7, LW), F32)], axis=0).astype(BF)
    peak, total, v = attend(
        a2r[0:LW, 0:HEADS], lv, ((fcol == lv) | (fcol == 8)) & at_zero, fkeys
    )
    v = v.reshape(EP, HP, LAT)
    twice = jnp.concatenate([v, v], axis=1)
    upper = iota(twice.shape, 1) >> 3
    for p in range(SL // 2):
        rows = bs[1, :, 16 * p : 16 * p + 16, :].astype(F32)
        bs[1, :, 16 * p : 16 * p + 16, :] = jnp.where(upper + 2 * p == lv, twice, rows).astype(BF)
    stat = bt[1].reshape(HEADS, 128)
    stat = jnp.where(group == 2 * lv, peak, jnp.where(group == 2 * lv + 1, total, stat))
    bt[1] = stat.reshape(EP, HP, 128)
    keep_own(1)
    for x in b_x[1]:
        x.start()

    head_of = iota((SL * HP, VD), 0) & (HP - 1)

    c_x = spread_dp(1, DP, lambda d: cs, lambda d: cr.at[d], scs, rcs)

    def merge(k):
        for x in b_x[k]:
            x.wait()
        stats = btr[k]
        w = jnp.exp(stats - jnp.max(stats, axis=0, keepdims=True))
        shifted = jnp.concatenate([stats[:, :, 16:], stats[:, :, :16]], axis=2)
        sc[...] = w / jnp.sum(w * shifted, axis=0, keepdims=True)

        def add(j, acc):
            one = sc[j]
            scale = jnp.concatenate([one[:, 32 * s : 32 * s + 1] for s in range(SL)], axis=0)
            return acc + scale * br[k, j].astype(F32)

        latent = lax.fori_loop(0, EP, add, jnp.zeros((SL * HP, LAT), F32)).astype(BF)
        values = jnp.zeros((SL * HP, VD), F32)
        for h in range(HP):
            values = jnp.where(head_of == h, dot(latent, vw[h]), values)
        values = values.astype(BF)
        vals[SL * HP * k : SL * HP * (k + 1)] = values

    loads[6].wait()
    merge(0)
    merge(1)

    together = vals[...]
    flat = []
    for h in range(HP):
        want = (iota((8, 2 * SL * HP), 0) >> 2) * (SL * HP) + (iota((8, 2 * SL * HP), 0) & 3) * HP + h
        chosen = jnp.where(iota((8, 2 * SL * HP), 1) == want, 1.0, 0.0).astype(BF)
        flat.append(dot(chosen, together))
    half = HP // 2
    flat = jnp.concatenate(
        [jnp.concatenate(flat[:half], axis=1), jnp.concatenate(flat[half:], axis=1)], axis=0
    ).astype(BF)
    cs[...] = flat
    cr[dp] = flat
    c_x.start()

    loads[10].wait()
    ow_x.wait()
    for h in range(HP):
        lines_of = [owr[d, VC * h : VC * (h + 1)].astype(F32) for d in range(DP)]
        owp[VD * h : VD * (h + 1)] = jnp.concatenate(lines_of, axis=0).astype(BF)

    own_rows = pl.ds(pl.multiple_of(core * HALF, 16), HALF)
    other_rows = pl.ds(pl.multiple_of((1 - core) * HALF, 16), HALF)
    odd = dp % 2 == 1

    def own_columns(part):
        return jnp.where(odd, part[:, WIN - BW :], part[:, :BW])

    c_x.wait()
    came = cr[...].astype(F32)
    came = jnp.concatenate([came[:, :8], came[:, 8:]], axis=2).reshape(ROWS, HP * VD)
    came = dot(place, came.astype(BF)).astype(BF)
    part = own_columns(dot(came, owp[...])).astype(BF)
    for g in range(EP // 2):
        for t in range(2):
            es1[2 * g + t] = part[16 * g : 16 * (g + 1), HB * t : HB * (t + 1)]
    er1[ep] = es1[ep]
    e_x = spread_ep(1, EP, lambda e: es1.at[e], lambda e: er1.at[e], s1, r1)
    e_x.start()
    e_x.wait()
    hidden = own_resid + jnp.sum(er1[...].astype(F32), axis=0)

    scaled = hidden * own_gain
    square = jnp.sum(hidden * hidden, axis=1, keepdims=True)
    hi = square.astype(BF).astype(F32)
    mid = (square - hi).astype(BF).astype(F32)
    lane = iota((16, 256 - HB), 1)
    extra = jnp.where(lane == 0, hi, jnp.where(lane == 1, mid, square - hi - mid))
    block = jnp.concatenate([scaled, extra], axis=1).astype(BF)
    gs[...] = block

    def rows_of(e):
        return pl.ds(pl.multiple_of((e // 2) * 16, 16), 16)

    hb[core, col_half, z, rows_of(ep)] = block
    gz_x = spread_z(lambda t: gs, lambda t: hb.at[core, col_half, t, rows_of(ep)], sgz, rgz)
    gz_x.start()
    gz_x.wait()

    def region(e, c):
        return hb.at[c, e % 2, :, rows_of(e)]

    gx_x = Exchange(
        moves, 1, EP,
        lambda i: remote(
            region(ep, core), region(ep, core), sgx.at[to_ep(i)], rgx.at[ep], dp, to_ep(i)
        ),
        lambda i: remote(
            region(ep, core), region(to_ep(EP - i), core), sgx.at[ep], rgx.at[to_ep(EP - i)], dp, ep
        ),
    )

    def gc_copy(e):
        return remote(region(e, core), region(e, core), sgc.at[e], rgc.at[e], sibling, ep)

    def gc_wait(e):
        other = region(e, 1 - core)
        remote(other, other, sgc.at[e], rgc.at[e], sibling, ep).wait_recv()

    gx_x.start()
    gc_copy(ep).start()
    loads[8].wait()
    loads[9].wait()

    def pass_on(i):
        gx_x.arrive(i).wait_recv()
        gc_copy(to_ep(EP - i)).start()

    loop(1, EP, pass_on)

    def project(t, acc):
        proj, squares = acc
        for c in range(2):
            for half in range(2):
                block = hb[c, half, t]
                w = gu[pl.ds(pl.multiple_of((2 * t + c) * BW + half * HB, 16), HB), :]
                proj = proj + dot(block[:, :HB], w)
                squares = squares + block[:, 128:].astype(F32)
        return proj, squares

    loop(0, EP, gc_wait)
    acc = (jnp.zeros((ROWS, 256), F32), jnp.zeros((ROWS, 128), F32))
    proj, squares = lax.fori_loop(0, NZ, project, acc)
    at = pl.ds(pl.multiple_of((core * NZ + z) // 2 * 16, 16), 16)
    sixteen = jnp.concatenate(
        [hb[ep % 2, t, ep // 2, at, :].astype(F32)[:, :HB] for t in range(2)], axis=1
    )
    hidden = jnp.where(z % 2 == 1, sixteen[8:], sixteen[:8]) / mixed_gain
    off = HB - 128
    square = squares[:, off : off + 1] + squares[:, off + 1 : off + 2] + squares[:, off + 2 : off + 3]
    scale = lax.rsqrt(square / float(BW * EP) + NORM_EPS)
    g = proj[:, :128] * scale
    u = proj[:, 128:] * scale
    act = (g / (1.0 + jnp.exp(-g)) * u * rw[:, 0:1]).astype(BF)
    loads[11].wait()

    def c_copy(j):
        return remote(pc.at[j, other_rows], pr.at[j], s2c.at[j], r2c.at[j], sibling, ep)

    def x_copy(j):
        return remote(xs.at[j], xr.at[ep], s2x.at[j], r2x.at[ep], dp, j)

    def pair(i):
        return (ep // 2 + 1 + i) % (EP // 2)

    def first(i):
        jp = pair(i)
        part = dot(act, dn[:, pl.ds(pl.multiple_of(jp * 2 * BW, 128), 2 * BW)])
        pc[2 * jp] = part[:, :BW].astype(BF)
        pc[2 * jp + 1] = part[:, BW:].astype(BF)
        c_copy(2 * jp).start()
        c_copy(2 * jp + 1).start()

    def second(i):
        for t in range(2):
            j = 2 * pair(i) + t
            c_copy(j).wait_recv()
            xs[j] = (pc[j, own_rows].astype(F32) + pr[j].astype(F32)).astype(BF)

            @pl.when(j != ep)
            def _():
                x_copy(j).start()

    def both(i):
        first(i)
        second(i - 1)

    first(0)
    loop(1, EP // 2, both)
    second(EP // 2 - 1)

    def x_sum(i, acc):
        j = to_ep(EP - i)
        remote(xs.at[j], xr.at[j], s2x.at[j], r2x.at[j], dp, j).wait_recv()
        return acc + xr[j].astype(F32)

    total = lax.fori_loop(1, EP, x_sum, xs[ep].astype(F32))
    total = total.reshape(NZ, 8, BW)
    zs[...] = jnp.concatenate([total[:, :, :HB], total[:, :, HB:]], axis=1).astype(BF)
    zr[z] = zs[z]
    z_x = spread_z(lambda t: zs.at[t], lambda t: zr.at[t], s2z, r2z)
    z_x.start()
    z_x.wait()
    total = jnp.sum(zr[...].astype(F32), axis=0)
    routed = jnp.concatenate([total[:8], total[8:]], axis=1)
    mixed = (hidden + routed).astype(out.dtype)
    out[0] = mixed[0:4]
    out[1] = mixed[4:8]

    for x in moves:
        x.finish()
    loop(0, EP, lambda e: gc_copy(e).wait_send())
    loop(0, EP, lambda j: c_copy(j).wait_send())
    loop(1, EP, lambda i: x_copy(to_ep(i)).wait_send())


def body(
    DP, EP,
    latent_cache, lengths, queries, fresh_latent, leaving, target, value_weight, output_weight,
    residual_stream, norm_gain, expert_ids, gate_codes, gate_weight, up_weight, down_weight,
):
    SL, T, LW = latent_cache.shape
    H = queries.shape[2]
    HP, _, VD = value_weight.shape
    D = norm_gain.shape[0]
    BW = D // EP
    NZ = DP // 2
    ROWS = DP * 8
    HALF = ROWS // 2
    PIECE = 768 // EP
    cache = jnp.swapaxes(latent_cache, 1, 2)
    q = jnp.swapaxes(queries, 2, 3)
    gain = norm_gain.astype(F32).reshape(D // 128, 128)
    ow = output_weight.reshape(HP * output_weight.shape[1], D)
    smem = pl.BlockSpec(memory_space=pltpu.SMEM)
    vmem = pl.BlockSpec(memory_space=pltpu.VMEM)
    anyw = pl.BlockSpec(memory_space=pl.ANY)
    V = pltpu.VMEM
    sems = lambda *n: pltpu.SemaphoreType.DMA(n)
    scratch = [
        V((SL, LW, H), BF), V((SL, LW, H), BF), V((SL, LW, T), BF), V(value_weight.shape, BF),
        V((D, 256), BF), V((2, 16, 2 * BW), BF),
        V((DP, ow.shape[0], BW + 64), BF),
        V((HP * VD, BW + 64), BF), V((2 * SL * HP, VD), BF), V((128, D), BF),
        V((768, 128), BF), V((2, NZ, PIECE, 128), BF), V((PIECE, 128), BF), V((768, 128), BF), V((16, LW), BF),
        V((2, EP, SL * HP, LAT), BF), V((2, EP, HP, 128), F32), V((2, EP, SL * HP, LAT), BF),
        V((2, EP, HP, 128), F32), V((EP, HP, 128), F32), V((SL * HP, LAT), BF),
        V((16, HP * VD // 2), BF), V((DP, 16, HP * VD // 2), BF),
        *[V((EP, 16, BW // 2), BF)] * 2,
        V((EP, ROWS, BW), BF), *[V((EP, HALF, BW), BF)] * 3, *[V((NZ, 16, BW // 2), BF)] * 2,
        V((16, 256), BF), V((2, 2, NZ, ROWS, 256), BF), V((ROWS, 128), F32),
        sems(12), sems(NZ), sems(NZ), pltpu.SemaphoreType.DMA, pltpu.SemaphoreType.DMA, sems(EP), sems(EP), sems(2, EP), sems(2, EP), sems(2, EP), sems(2, EP),
        sems(DP), sems(DP),
        sems(DP), sems(DP), *[sems(EP)] * 2, *[sems(EP)] * 4, *[sems(NZ)] * 2,
        sems(NZ), sems(NZ), sems(EP), sems(EP), sems(EP), sems(EP),
    ]
    return pl.pallas_call(
        functools.partial(kernel, DP, EP),
        out_shape=jax.ShapeDtypeStruct((2, SL, BW), BF),
        in_specs=[smem] * 3 + [vmem] * 4 + [anyw] * 8,
        out_specs=vmem,
        scratch_shapes=scratch,
        compiler_params=pltpu.CompilerParams(
            collective_id=0, has_side_effects=True, vmem_limit_bytes=56 * 2**20
        ),
        name="decode",
    )(
        lengths, leaving, target, fresh_latent,
        jnp.swapaxes(expert_ids, 1, 2), jnp.swapaxes(gate_codes, 1, 2), gain, residual_stream,
        cache, q, value_weight, ow, gate_weight[0], up_weight[0], down_weight[0],
    )


def solution(mesh):
    placed = (
        P("dp", "ep", None), P(), P(None, "dp", None, None), P(None, "dp", None), P(), P(),
        P("ep", None, None), P("ep", "dp", None), P(), P(), P(), P(),
        P("ep", None, "dp"), P("ep", None, "dp"), P("ep", "dp", None),
    )
    return jax.shard_map(
        functools.partial(body, mesh.shape["dp"], mesh.shape["ep"]),
        mesh=mesh, in_specs=placed, out_specs=P(None, "dp", "ep"), check_vma=False,
    )
```

```python
import functools

import jax
import jax.numpy as jnp
from jax import lax
from jax.experimental import pallas as pl
from jax.experimental.pallas import tpu as pltpu
from jax.sharding import PartitionSpec as P

MESH = pl.DeviceIdType.MESH
SCORE_SCALE = 192.0 ** (-0.5)
ROUTE_SCALE = 2.5
NORM_EPS = 1e-06
MASKED = -1e30
LAT = 512
BF = jnp.bfloat16
F32 = jnp.float32


def iota(shape, dim):
    return lax.broadcasted_iota(jnp.int32, shape, dim)


def dot(a, b, ca=1, cb=0):
    return lax.dot_general(a, b, (((ca,), (cb,)), ((), ())), preferred_element_type=F32)


def loop(lo, hi, fn):
    lax.fori_loop(lo, hi, lambda i, c: (fn(i), c)[1], 0)


class Exchange:
    def __init__(self, moves, lo, hi, copy, arrive):
        self.lo, self.hi, self.copy, self.arrive = lo, hi, copy, arrive
        moves.append(self)

    def start(self):
        loop(self.lo, self.hi, lambda i: self.copy(i).start())

    def wait(self):
        loop(self.lo, self.hi, lambda i: self.arrive(i).wait_recv())

    def finish(self):
        loop(self.lo, self.hi, lambda i: self.copy(i).wait_send())


def kernel(
    DP, EP,
    lengths, leaving, target, fresh, ids, codes, gain, resid,
    cache_h, q_h, vw_h, ow_h, gate_h, up_h, down_h,
    out,
    q1v, q2v, cv, vw, gu, rv,
    owr, owp, dn,
    a1s, a1r, a2s, a2r, fk,
    bs, bt, br, btr, sc, lat,
    cs, cr,
    es1, er1, pc, pr, xs, xr, zs, zr,
    gs, hb, rw,
    ld, sa1, ra1, sa1c, ra1c, sa2, ra2, sb, rb, st, rt, scs, rcs,
    sow, row_, s1, r1,
    s2c, r2c, s2x, r2x, s2z, r2z,
    sgz, rgz, sgx, rgx, sgc, rgc, sga, rga, sgb, rgb,
):
    NZ = DP // 2
    SL = 4
    HP = vw.shape[0] * 2
    VD = vw.shape[2] // 2
    VC = VD // DP
    ROWS = DP * 8
    HALF = ROWS // 2
    BW = owr.shape[2] - 64
    WIN = owr.shape[2]
    HB = BW // 2
    LW = cv.shape[1]
    T = cv.shape[2]
    HEADS = q1v.shape[2]
    PIECE = a2s.shape[0]
    dp = lax.axis_index("dp")
    ep = lax.axis_index("ep")
    z = dp // 2
    core = dp % 2
    sibling = z * 2 + (1 - core)

    def to_dp(k):
        return (dp + k) % DP

    def to_ep(k):
        return (ep + k) % EP

    def remote(src, dst, s, r, d, e):
        return pltpu.make_async_remote_copy(
            src_ref=src, dst_ref=dst, send_sem=s, recv_sem=r, device_id=(d, e), device_id_type=MESH
        )

    moves = []

    def spread_dp(lo, hi, src, dst, s, r):
        def copy(i):
            d = to_dp(i)
            return remote(src(d), dst(dp), s.at[d], r.at[dp], d, ep)

        def arrive(i):
            d = to_dp(DP - i)
            return remote(src(d), dst(d), s.at[d], r.at[d], d, ep)

        return Exchange(moves, lo, hi, copy, arrive)

    def spread_ep(lo, hi, src, dst, s, r):
        def copy(i):
            e = to_ep(i)
            return remote(src(e), dst(ep), s.at[e], r.at[ep], dp, e)

        def arrive(i):
            e = to_ep(EP - i)
            return remote(src(e), dst(e), s.at[e], r.at[e], dp, e)

        return Exchange(moves, lo, hi, copy, arrive)

    def local(src, dst, k):
        return pltpu.make_async_copy(src, dst, ld.at[k])

    def window(e):
        start = (e // 2) * 2 * BW + (e % 2) * (2 * BW - WIN)
        return pl.ds(pl.multiple_of(start, 128), WIN)

    row_group = ep // 2
    col_half = ep % 2
    first_core, first_z = (2 * row_group) // NZ, (2 * row_group) % NZ
    pair_cols = pl.ds(pl.multiple_of((dp // 2) * 2 * BW, 128), 2 * BW)
    group_rows = pl.ds(pl.multiple_of(first_z * 8, 16), 16)
    loads = [local(q_h.at[1], q2v, 0), local(q_h.at[0], q1v, 1)]
    loads += [local(cache_h.at[s], cv.at[s], 2 + s) for s in range(SL)]
    loads += [
        local(resid.at[:, group_rows, pair_cols], rv, 7),
        local(gate_h, gu.at[:, pl.ds(0, 128)], 8),
        local(up_h, gu.at[:, pl.ds(128, 128)], 9),
        local(ow_h.at[:, window(dp)], owr.at[dp], 10),
        local(down_h, dn, 11),
    ]
    loads[0].start()
    pairs = [
        local(vw_h.at[h], vw.at[h // 2, :, pl.ds((h % 2) * VD, VD)], 12 + h) for h in range(HP)
    ]

    barrier = pltpu.get_barrier_semaphore()
    loop(1, DP, lambda k: pl.semaphore_signal(barrier, inc=1, device_id=(to_dp(k), ep), device_id_type=MESH))
    loop(1, EP, lambda k: pl.semaphore_signal(barrier, inc=1, device_id=(dp, to_ep(k)), device_id_type=MESH))

    lv = leaving[dp]
    f0 = fresh[0].astype(F32)
    f1 = fresh[1].astype(F32)
    frow = jnp.sum(jnp.where(iota(f1.shape, 0) == lv, f1, 0.0), axis=0, keepdims=True)
    frow = jnp.concatenate([frow, jnp.zeros((1, 640 - LW), F32)], axis=1)
    fpieces = [frow[:, 128 * i : 128 * (i + 1)] for i in range(5)]
    loads[0].wait()
    a1s[0:LW, 0:HEADS] = q2v[lv]
    a1s[LW : LW + 16] = jnp.concatenate(fpieces + [jnp.zeros((11, 128), F32)], axis=0).astype(BF)
    a1s[LW + 16 :] = jnp.zeros((a1s.shape[0] - LW - 16, 128), BF)
    mine = pl.ds(pl.multiple_of(ep * PIECE, 16), PIECE)
    a1r[core, z] = a1s[mine]
    pl.semaphore_wait(barrier, DP + EP - 2)

    def spread_z(src, dst, s, r):
        def copy(i):
            t = (z + i) % NZ
            return remote(src(t), dst(z), s.at[t], r.at[z], t * 2 + core, ep)

        def arrive(i):
            t = (z + NZ - i) % NZ
            return remote(src(t), dst(t), s.at[t], r.at[t], t * 2 + core, ep)

        return Exchange(moves, 1, NZ, copy, arrive)

    a1 = spread_z(lambda t: a1s.at[mine], lambda t: a1r.at[core, t], sa1, ra1)
    a1.start()
    for c in loads[1:6] + pairs + loads[6:]:
        c.start()

    ow_x = spread_dp(1, DP, lambda d: ow_h.at[:, window(d)], lambda d: owr.at[d], sow, row_)

    def attend(q, s, live_fresh, fkeys):
        kt = cv[s]
        score = dot(q, kt, 0, 0) * SCORE_SCALE
        pos = ep * T + iota(score.shape, 1)
        live = pos < lengths[dp * SL + s]
        fscore = dot(q, fkeys, 0, 1) * SCORE_SCALE
        score = jnp.where(live, score, MASKED)
        fscore = jnp.where(live_fresh, fscore, MASKED)
        peak = jnp.maximum(
            jnp.max(score, axis=1, keepdims=True), jnp.max(fscore, axis=1, keepdims=True)
        )
        w = jnp.where(live, jnp.exp(score - peak), 0.0)
        fw = jnp.where(live_fresh, jnp.exp(fscore - peak), 0.0)
        total = jnp.sum(w, axis=1, keepdims=True) + jnp.sum(fw, axis=1, keepdims=True)
        v = dot(w.astype(BF), kt[:LAT], 1, 1) + dot(fw.astype(BF), fkeys[:, :LAT])
        return peak, total, v

    group = iota((HEADS, 128), 1) >> 4

    def attend_step(k, query_of, live_of):
        stat = jnp.zeros((HEADS, 128), F32)
        for p in range(SL // 2):
            both = []
            for s in (2 * p, 2 * p + 1):
                peak, total, v = attend(query_of(s), s, live_of(s), fk[...])
                stat = jnp.where(group == 2 * s, peak, jnp.where(group == 2 * s + 1, total, stat))
                both.append(v.reshape(EP, HP, LAT))
            bs[k, :, 16 * p : 16 * p + 16, :] = jnp.concatenate(both, axis=1).astype(BF)
        bt[k] = stat.reshape(EP, HP, 128)

    def keep_own(k):
        br[k, ep] = bs[k, ep]
        btr[k, ep] = bt[k, ep]

    def partial_exchange(k):
        return (
            spread_ep(1, EP, lambda e: bt.at[k, e], lambda e: btr.at[k, e], st.at[k], rt.at[k]),
            spread_ep(1, EP, lambda e: bs.at[k, e], lambda e: br.at[k, e], sb.at[k], rb.at[k]),
        )

    b_x = [partial_exchange(0), partial_exchange(1)]

    fcol = iota((1, 16), 1)
    at_zero = ep == 0
    fk[...] = jnp.concatenate([f0, f1, jnp.zeros((8, LW), F32)], axis=0).astype(BF)
    loads[1].wait()
    for s in range(SL):
        loads[2 + s].wait()
    attend_step(0, lambda s: q1v[s], lambda s: (fcol == s) & at_zero)
    keep_own(0)

    a1.wait()
    a1c = Exchange(
        moves, 0, 1,
        lambda i: remote(a1r.at[core], a1r.at[core], sa1c, ra1c, sibling, ep),
        lambda i: remote(a1r.at[1 - core], a1r.at[1 - core], sa1c, ra1c, sibling, ep),
    )
    a1c.start()
    a1c.wait()
    ow_x.start()
    other = target[dp]
    piece = a1r[other & 1, other >> 1]
    a2s[...] = piece
    a2r[mine] = piece

    def piece_rows(e):
        return a2r.at[pl.ds(pl.multiple_of(e * PIECE, 16), PIECE)]

    a2 = spread_ep(1, EP, lambda e: a2s, piece_rows, sa2, ra2)
    a2.start()
    for x in b_x[0]:
        x.start()

    row = iota((ROWS, 2 * SL * DP), 0)
    col = iota((ROWS, 2 * SL * DP), 1)
    half_bits = HALF.bit_length() - 1
    r_core = row >> half_bits
    r_z = (row >> 3) & (NZ - 1)
    r_step = (row >> 2) & 1
    slot = (r_z * 2 + r_core) * SL + (row & 3)
    held = slot
    for r in range(DP):
        t = target[r]
        held = jnp.where(slot == t * SL + leaving[t], r * SL + leaving[r], held)
    held = jnp.where(r_step == 1, held, slot)
    place = ((held >> 2) * 8 + r_step * 4 + (held & 3)) == col
    code = codes[...].astype(F32)
    share = code / jnp.sum(code, axis=1, keepdims=True) * ROUTE_SCALE
    weight = jnp.sum(jnp.where(ids[...] == ep, share, 0.0), axis=1)
    weight = jnp.concatenate([weight[0:1], weight[1:2]], axis=1)
    own_place = (r_step * (SL * DP) + slot) == col
    rw[...] = jnp.broadcast_to(
        jnp.sum(jnp.where(own_place, weight, 0.0), axis=1, keepdims=True), (ROWS, 128)
    )
    place = jnp.where(place, 1.0, 0.0).astype(BF)
    lines = 2 * BW // 128
    seven = jnp.zeros((lines, 128), F32)
    mixed_gain = jnp.zeros((lines, 128), F32)
    for i in range(EP // 2):
        seven = jnp.where(dp // 2 == i, gain[lines * i : lines * (i + 1)], seven)
        mixed_gain = jnp.where(ep // 2 == i, gain[lines * i : lines * (i + 1)], mixed_gain)
    seven = jnp.concatenate([seven[i : i + 1] for i in range(lines)], axis=1)
    mixed_gain = jnp.concatenate([mixed_gain[i : i + 1] for i in range(lines)], axis=1)
    mixed_gain = jnp.where(ep % 2 == 1, mixed_gain[:, BW:], mixed_gain[:, :BW])

    def quarter(wide):
        out = wide[:, :HB]
        for i in range(1, 4):
            out = jnp.where((dp % 2) * 2 + col_half == i, wide[:, HB * i : HB * (i + 1)], out)
        return out

    own_gain = quarter(seven)
    loads[6].wait()
    wide = rv[...].astype(F32)
    own_resid = [
        jnp.where(first_core == 0, wide[k, 8 * t : 8 * t + 4], wide[k, 8 * t + 4 : 8 * t + 8])
        for t in range(2)
        for k in range(2)
    ]
    own_resid = quarter(jnp.concatenate(own_resid, axis=0))

    attend_step(1, lambda s: q2v[s], lambda s: ((fcol == s) | (fcol == 4 + s)) & at_zero)
    a2.wait()
    moved_f = a2r[LW : LW + 16].astype(F32)
    moved_f = jnp.concatenate([moved_f[i : i + 1] for i in range(5)], axis=1)[:, :LW]
    fkeys = jnp.concatenate([f0, f1, moved_f, jnp.zeros((7, LW), F32)], axis=0).astype(BF)
    peak, total, v = attend(
        a2r[0:LW, 0:HEADS], lv, ((fcol == lv) | (fcol == 8)) & at_zero, fkeys
    )
    v = v.reshape(EP, HP, LAT)
    twice = jnp.concatenate([v, v], axis=1)
    upper = iota(twice.shape, 1) >> 3
    for p in range(SL // 2):
        rows = bs[1, :, 16 * p : 16 * p + 16, :].astype(F32)
        bs[1, :, 16 * p : 16 * p + 16, :] = jnp.where(upper + 2 * p == lv, twice, rows).astype(BF)
    stat = bt[1].reshape(HEADS, 128)
    stat = jnp.where(group == 2 * lv, peak, jnp.where(group == 2 * lv + 1, total, stat))
    bt[1] = stat.reshape(EP, HP, 128)
    keep_own(1)
    for x in b_x[1]:
        x.start()

    head_of = iota((SL * HP, VD), 0) & (HP - 1)

    c_x = [
        spread_dp(1, DP, lambda d, k=k: cs.at[k], lambda d, k=k: cr.at[k, d], scs.at[k], rcs.at[k])
        for k in range(2)
    ]

    def merge(k):
        for x in b_x[k]:
            x.wait()
        stats = btr[k]
        w = jnp.exp(stats - jnp.max(stats, axis=0, keepdims=True))
        shifted = jnp.concatenate([stats[:, :, 16:], stats[:, :, :16]], axis=2)
        sc[...] = w / jnp.sum(w * shifted, axis=0, keepdims=True)

        def add(j, acc):
            one = sc[j]
            scale = jnp.concatenate([one[:, 32 * s : 32 * s + 1] for s in range(SL)], axis=0)
            return acc + scale * br[k, j].astype(F32)

        latent = lax.fori_loop(0, EP, add, jnp.zeros((SL * HP, LAT), F32)).astype(BF)
        values = jnp.zeros((SL * HP, VD), F32)
        for p in range(HP // 2):
            two = dot(latent, vw[p])
            values = jnp.where(head_of == 2 * p, two[:, :VD], values)
            values = jnp.where(head_of == 2 * p + 1, two[:, VD:], values)
        values = values.astype(BF)
        flat = []
        for h in range(HP):
            want = iota((SL, SL * HP), 0) * HP + h
            flat.append(dot(jnp.where(iota((SL, SL * HP), 1) == want, 1.0, 0.0).astype(BF), values))
        few = HP // 4
        flat = [jnp.concatenate(flat[few * t : few * (t + 1)], axis=1) for t in range(4)]
        flat = jnp.concatenate(flat, axis=0).astype(BF)
        cs[k] = flat
        cr[k, dp] = flat
        c_x[k].start()

    for c in pairs:
        c.wait()
    merge(0)
    merge(1)

    loads[9].wait()
    ow_x.wait()
    for h in range(HP):
        lines_of = [owr[d, VC * h : VC * (h + 1)].astype(F32) for d in range(DP)]
        owp[VD * h : VD * (h + 1)] = jnp.concatenate(lines_of, axis=0).astype(BF)

    own_rows = pl.ds(pl.multiple_of(core * HALF, 16), HALF)
    other_rows = pl.ds(pl.multiple_of((1 - core) * HALF, 16), HALF)
    odd = dp % 2 == 1

    def own_columns(part):
        return jnp.where(odd, part[:, WIN - BW :], part[:, :BW])

    came = []
    for k in range(2):
        c_x[k].wait()
        one = cr[k].astype(F32)
        came.append(jnp.concatenate([one[:, SL * t : SL * (t + 1)] for t in range(4)], axis=2))
    came = jnp.concatenate(came, axis=1).reshape(ROWS, HP * VD)
    came = dot(place, came.astype(BF)).astype(BF)
    part = own_columns(dot(came, owp[...])).astype(BF)
    for g in range(EP // 2):
        for t in range(2):
            es1[2 * g + t] = part[16 * g : 16 * (g + 1), HB * t : HB * (t + 1)]
    er1[ep] = es1[ep]
    e_x = spread_ep(1, EP, lambda e: es1.at[e], lambda e: er1.at[e], s1, r1)
    e_x.start()
    e_x.wait()
    hidden = own_resid + jnp.sum(er1[...].astype(F32), axis=0)

    scaled = hidden * own_gain
    square = jnp.sum(hidden * hidden, axis=1, keepdims=True)
    hi = square.astype(BF).astype(F32)
    mid = (square - hi).astype(BF).astype(F32)
    lane = iota((16, 256 - HB), 1)
    extra = jnp.where(lane == 0, hi, jnp.where(lane == 1, mid, square - hi - mid))
    block = jnp.concatenate([scaled, extra], axis=1).astype(BF)
    gs[...] = block

    def rows_of(e):
        return pl.ds(pl.multiple_of((e // 2) * 16, 16), 16)

    hb[core, col_half, z, rows_of(ep)] = block
    gz_x = spread_z(lambda t: gs, lambda t: hb.at[core, col_half, t, rows_of(ep)], sgz, rgz)
    gz_x.start()
    gz_x.wait()

    def region(e, c):
        return hb.at[c, e % 2, :, rows_of(e)]

    def region_half(e, h):
        return hb.at[core, e % 2, pl.ds(h * (NZ // 2), NZ // 2), rows_of(e)]

    NX = 4 if EP == 16 else 2
    NY = EP // NX
    y, x = ep // NX, ep % NX

    def on_x(i):
        return y * NX + (x + i) % NX

    def on_y(i):
        return ((y + i) % NY) * NX + x

    def whole(e):
        return remote(region(ep, core), region(ep, core), sgx.at[e], rgx.at[ep], dp, e)

    def whole_wait(e):
        remote(region(e, core), region(e, core), sgx.at[e], rgx.at[e], dp, e).wait_recv()

    def first_on(i, j):
        e = on_x(NX - i)
        half = region_half(e, 0)
        return remote(half, half, sga.at[i, j], rga.at[e], dp, on_y(j))

    def second_on(i, j):
        e = on_y(NY - i)
        half = region_half(e, 1)
        return remote(half, half, sgb.at[i, j], rgb.at[e], dp, on_x(j))

    def gc_copy(e):
        return remote(region(e, core), region(e, core), sgc.at[e], rgc.at[e], sibling, ep)

    def gc_wait(e):
        other = region(e, 1 - core)
        remote(other, other, sgc.at[e], rgc.at[e], sibling, ep).wait_recv()

    loop(1, NX, lambda i: whole(on_x(i)).start())
    loop(1, NY, lambda i: whole(on_y(i)).start())
    gc_copy(ep).start()
    loads[7].wait()
    loads[8].wait()

    def pass_x(i):
        whole_wait(on_x(NX - i))
        loop(1, NY, lambda j: first_on(i, j).start())
        gc_copy(on_x(NX - i)).start()

    def pass_y(i):
        whole_wait(on_y(NY - i))
        loop(1, NX, lambda j: second_on(i, j).start())
        gc_copy(on_y(NY - i)).start()

    def across(n):
        e = ((y + 1 + n // (NX - 1)) % NY) * NX + (x + 1 + n % (NX - 1)) % NX
        first, second = region_half(e, 0), region_half(e, 1)
        remote(first, first, sga.at[0, 0], rga.at[e], dp, e).wait_recv()
        remote(second, second, sgb.at[0, 0], rgb.at[e], dp, e).wait_recv()
        gc_copy(e).start()

    for i in range(1, max(NX, NY)):
        if i < NX:
            pass_x(i)
        if i < NY:
            pass_y(i)
    loop(0, (NX - 1) * (NY - 1), across)

    def project(t, acc):
        proj, squares = acc
        for c in range(2):
            for half in range(2):
                block = hb[c, half, t]
                w = gu[pl.ds(pl.multiple_of((2 * t + c) * BW + half * HB, 16), HB), :]
                proj = proj + dot(block[:, :HB], w)
                squares = squares + block[:, 128:].astype(F32)
        return proj, squares

    loop(0, EP, gc_wait)
    acc = (jnp.zeros((ROWS, 256), F32), jnp.zeros((ROWS, 128), F32))
    proj, squares = lax.fori_loop(0, NZ, project, acc)
    at = pl.ds(pl.multiple_of((core * NZ + z) // 2 * 16, 16), 16)
    sixteen = jnp.concatenate(
        [hb[ep % 2, t, ep // 2, at, :].astype(F32)[:, :HB] for t in range(2)], axis=1
    )
    hidden = jnp.where(z % 2 == 1, sixteen[8:], sixteen[:8]) / mixed_gain
    off = HB - 128
    square = squares[:, off : off + 1] + squares[:, off + 1 : off + 2] + squares[:, off + 2 : off + 3]
    scale = lax.rsqrt(square / float(BW * EP) + NORM_EPS)
    g = proj[:, :128] * scale
    u = proj[:, 128:] * scale
    act = (g / (1.0 + jnp.exp(-g)) * u * rw[:, 0:1]).astype(BF)
    loads[10].wait()

    def c_copy(j):
        return remote(pc.at[j, other_rows], pr.at[j], s2c.at[j], r2c.at[j], sibling, ep)

    def x_copy(j):
        return remote(xs.at[j], xr.at[ep], s2x.at[j], r2x.at[ep], dp, j)

    def pair(i):
        return (ep // 2 + 1 + i) % (EP // 2)

    def first(i):
        jp = pair(i)
        part = dot(act, dn[:, pl.ds(pl.multiple_of(jp * 2 * BW, 128), 2 * BW)])
        pc[2 * jp] = part[:, :BW].astype(BF)
        pc[2 * jp + 1] = part[:, BW:].astype(BF)
        c_copy(2 * jp).start()
        c_copy(2 * jp + 1).start()

    def second(i):
        for t in range(2):
            j = 2 * pair(i) + t
            c_copy(j).wait_recv()
            part = pc[j, own_rows].astype(F32) + pr[j].astype(F32)
            tail = part[:, BW - 64 :]
            tail = jnp.concatenate([tail[: HALF // 2], tail[HALF // 2 :]], axis=1)
            tiles = [part[:, 128 * i : 128 * (i + 1)] for i in range(BW // 128)]
            xs[j] = jnp.concatenate(tiles + [tail], axis=0).astype(BF)

            @pl.when(j != ep)
            def _():
                x_copy(j).start()

    def both(i):
        first(i)
        second(i - 1)

    first(0)
    loop(1, EP // 2, both)
    second(EP // 2 - 1)

    def x_sum(i, acc):
        j = to_ep(EP - i)
        remote(xs.at[j], xr.at[j], s2x.at[j], r2x.at[j], dp, j).wait_recv()
        return acc + xr[j].astype(F32)

    total = lax.fori_loop(1, EP, x_sum, xs[ep].astype(F32))
    tail = total[HALF * (BW // 128) :]
    tail = jnp.concatenate([tail[:, :64], tail[:, 64:]], axis=0)
    tiles = [total[HALF * i : HALF * (i + 1)] for i in range(BW // 128)]
    total = jnp.concatenate(tiles + [tail], axis=1).reshape(NZ, 8, BW)
    zs[...] = jnp.concatenate([total[:, :, :HB], total[:, :, HB:]], axis=1).astype(BF)
    zr[z] = zs[z]
    z_x = spread_z(lambda t: zs.at[t], lambda t: zr.at[t], s2z, r2z)
    z_x.start()
    z_x.wait()
    total = jnp.sum(zr[...].astype(F32), axis=0)
    routed = jnp.concatenate([total[:8], total[8:]], axis=1)
    mixed = (hidden + routed).astype(out.dtype)
    out[0] = mixed[0:4]
    out[1] = mixed[4:8]

    for move in moves:
        move.finish()
    loop(1, NX, lambda i: whole(on_x(i)).wait_send())
    loop(1, NY, lambda i: whole(on_y(i)).wait_send())
    for i in range(1, NX):
        loop(1, NY, lambda j: first_on(i, j).wait_send())
    for i in range(1, NY):
        loop(1, NX, lambda j: second_on(i, j).wait_send())
    loop(0, EP, lambda e: gc_copy(e).wait_send())
    loop(0, EP, lambda j: c_copy(j).wait_send())
    loop(1, EP, lambda i: x_copy(to_ep(i)).wait_send())


def body(
    DP, EP,
    latent_cache, lengths, queries, fresh_latent, leaving, target, value_weight, output_weight,
    residual_stream, norm_gain, expert_ids, gate_codes, gate_weight, up_weight, down_weight,
):
    SL, T, LW = latent_cache.shape
    H = queries.shape[2]
    HP, _, VD = value_weight.shape
    D = norm_gain.shape[0]
    BW = D // EP
    NZ = DP // 2
    ROWS = DP * 8
    HALF = ROWS // 2
    PIECE = 768 // EP
    cache = jnp.swapaxes(latent_cache, 1, 2)
    q = jnp.swapaxes(queries, 2, 3)
    gain = norm_gain.astype(F32).reshape(D // 128, 128)
    ow = output_weight.reshape(HP * output_weight.shape[1], D)
    smem = pl.BlockSpec(memory_space=pltpu.SMEM)
    vmem = pl.BlockSpec(memory_space=pltpu.VMEM)
    anyw = pl.BlockSpec(memory_space=pl.ANY)
    V = pltpu.VMEM
    sems = lambda *n: pltpu.SemaphoreType.DMA(n)
    scratch = [
        V((SL, LW, H), BF), V((SL, LW, H), BF), V((SL, LW, T), BF), V((HP // 2, value_weight.shape[1], 2 * VD), BF),
        V((D, 256), BF), V((2, 16, 2 * BW), BF),
        V((DP, ow.shape[0], BW + 64), BF),
        V((HP * VD, BW + 64), BF), V((128, D), BF),
        V((768, 128), BF), V((2, NZ, PIECE, 128), BF), V((PIECE, 128), BF), V((768, 128), BF), V((16, LW), BF),
        V((2, EP, SL * HP, LAT), BF), V((2, EP, HP, 128), F32), V((2, EP, SL * HP, LAT), BF),
        V((2, EP, HP, 128), F32), V((EP, HP, 128), F32), V((SL * HP, LAT), BF),
        V((2, 16, HP * VD // 4), BF), V((2, DP, 16, HP * VD // 4), BF),
        *[V((EP, 16, BW // 2), BF)] * 2,
        V((EP, ROWS, BW), BF), V((EP, HALF, BW), BF), *[V((EP, HALF * BW // 128, 128), BF)] * 2, *[V((NZ, 16, BW // 2), BF)] * 2,
        V((16, 256), BF), V((2, 2, NZ, ROWS, 256), BF), V((ROWS, 128), F32),
        sems(12 + HP), sems(NZ), sems(NZ), pltpu.SemaphoreType.DMA, pltpu.SemaphoreType.DMA, sems(EP), sems(EP), sems(2, EP), sems(2, EP), sems(2, EP), sems(2, EP),
        sems(2, DP), sems(2, DP),
        sems(DP), sems(DP), *[sems(EP)] * 2, *[sems(EP)] * 4, *[sems(NZ)] * 2,
        sems(NZ), sems(NZ), sems(EP), sems(EP), sems(EP), sems(EP), sems(4, 4), sems(EP), sems(4, 4), sems(EP),
    ]
    return pl.pallas_call(
        functools.partial(kernel, DP, EP),
        out_shape=jax.ShapeDtypeStruct((2, SL, BW), BF),
        in_specs=[smem] * 3 + [vmem] * 4 + [anyw] * 8,
        out_specs=vmem,
        scratch_shapes=scratch,
        compiler_params=pltpu.CompilerParams(
            collective_id=0, has_side_effects=True, vmem_limit_bytes=56 * 2**20
        ),
        name="decode",
    )(
        lengths, leaving, target, fresh_latent,
        jnp.swapaxes(expert_ids, 1, 2), jnp.swapaxes(gate_codes, 1, 2), gain, residual_stream,
        cache, q, value_weight, ow, gate_weight[0], up_weight[0], down_weight[0],
    )


def solution(mesh):
    placed = (
        P("dp", "ep", None), P(), P(None, "dp", None, None), P(None, "dp", None), P(), P(),
        P("ep", None, None), P("ep", "dp", None), P(), P(), P(), P(),
        P("ep", None, "dp"), P("ep", None, "dp"), P("ep", "dp", None),
    )
    return jax.shard_map(
        functools.partial(body, mesh.shape["dp"], mesh.shape["ep"]),
        mesh=mesh, in_specs=placed, out_specs=P(None, "dp", "ep"), check_vma=False,
    )
```

```python
import functools

import jax
import jax.numpy as jnp
from jax import lax
from jax.experimental import pallas as pl
from jax.experimental.pallas import tpu as pltpu
from jax.sharding import PartitionSpec as P

MESH = pl.DeviceIdType.MESH
SCORE_SCALE = 192.0 ** (-0.5)
ROUTE_SCALE = 2.5
NORM_EPS = 1e-06
MASKED = -1e30
LAT = 512
BF = jnp.bfloat16
F32 = jnp.float32


def iota(shape, dim):
    return lax.broadcasted_iota(jnp.int32, shape, dim)


def dot(a, b, ca=1, cb=0):
    return lax.dot_general(a, b, (((ca,), (cb,)), ((), ())), preferred_element_type=F32)


def loop(lo, hi, fn):
    lax.fori_loop(lo, hi, lambda i, c: (fn(i), c)[1], 0)


class Exchange:
    def __init__(self, moves, lo, hi, copy, arrive):
        self.lo, self.hi, self.copy, self.arrive = lo, hi, copy, arrive
        moves.append(self)

    def start(self):
        loop(self.lo, self.hi, lambda i: self.copy(i).start())

    def wait(self):
        loop(self.lo, self.hi, lambda i: self.arrive(i).wait_recv())

    def finish(self):
        loop(self.lo, self.hi, lambda i: self.copy(i).wait_send())


def kernel(
    DP, EP,
    lengths, leaving, target, fresh, ids, codes, gain, resid,
    cache_h, q_h, vw_h, ow_h, gate_h, up_h, down_h,
    out,
    q1v, q2v, cv, vw, gu, rv,
    owr, owp, dn,
    a1s, a1r, a2s, a2r, fk,
    bs, bt, br, btr, sc, lat,
    cs, cr,
    es1, er1, pc, pr, xs, xr, zs, zr,
    gs, hb, rw,
    ld, sa1, ra1, sa1c, ra1c, sa2, ra2, sb, rb, st, rt, scs, rcs,
    sow, row_, s1, r1,
    s2c, r2c, s2x, r2x, s2z, r2z,
    sgz, rgz, sgx, rgx, sgc, rgc, sga, rga, sgb, rgb,
):
    NZ = DP // 2
    SL = 4
    HP = vw.shape[0] * 2
    VD = vw.shape[2] // 2
    VC = VD // DP
    ROWS = DP * 8
    HALF = ROWS // 2
    BW = owr.shape[2] - 64
    WIN = owr.shape[2]
    HB = BW // 2
    LW = cv.shape[1]
    T = cv.shape[2]
    HEADS = q1v.shape[2]
    PIECE = a2s.shape[0]
    dp = lax.axis_index("dp")
    ep = lax.axis_index("ep")
    z = dp // 2
    core = dp % 2
    sibling = z * 2 + (1 - core)

    def to_dp(k):
        return (dp + k) % DP

    def to_ep(k):
        return (ep + k) % EP

    def remote(src, dst, s, r, d, e):
        return pltpu.make_async_remote_copy(
            src_ref=src, dst_ref=dst, send_sem=s, recv_sem=r, device_id=(d, e), device_id_type=MESH
        )

    moves = []

    def spread_dp(lo, hi, src, dst, s, r):
        def copy(i):
            d = to_dp(i)
            return remote(src(d), dst(dp), s.at[d], r.at[dp], d, ep)

        def arrive(i):
            d = to_dp(DP - i)
            return remote(src(d), dst(d), s.at[d], r.at[d], d, ep)

        return Exchange(moves, lo, hi, copy, arrive)

    def spread_ep(lo, hi, src, dst, s, r):
        def copy(i):
            e = to_ep(i)
            return remote(src(e), dst(ep), s.at[e], r.at[ep], dp, e)

        def arrive(i):
            e = to_ep(EP - i)
            return remote(src(e), dst(e), s.at[e], r.at[e], dp, e)

        return Exchange(moves, lo, hi, copy, arrive)

    def local(src, dst, k):
        return pltpu.make_async_copy(src, dst, ld.at[k])

    def window(e):
        start = (e // 2) * 2 * BW + (e % 2) * (2 * BW - WIN)
        return pl.ds(pl.multiple_of(start, 128), WIN)

    row_group = ep // 2
    col_half = ep % 2
    first_core, first_z = (2 * row_group) // NZ, (2 * row_group) % NZ
    pair_cols = pl.ds(pl.multiple_of((dp // 2) * 2 * BW, 128), 2 * BW)
    group_rows = pl.ds(pl.multiple_of(first_z * 8, 16), 16)
    loads = [local(q_h.at[1], q2v, 0), local(q_h.at[0], q1v, 1)]
    loads += [local(cache_h.at[s], cv.at[s], 2 + s) for s in range(SL)]
    loads += [
        local(resid.at[:, group_rows, pair_cols], rv, 7),
        local(gate_h, gu.at[:, pl.ds(0, 128)], 8),
        local(up_h, gu.at[:, pl.ds(128, 128)], 9),
        local(ow_h.at[:, window(dp)], owr.at[dp], 10),
        local(down_h, dn, 11),
    ]
    loads[0].start()
    pairs = [
        local(vw_h.at[h], vw.at[h // 2, :, pl.ds((h % 2) * VD, VD)], 12 + h) for h in range(HP)
    ]

    barrier = pltpu.get_barrier_semaphore()
    loop(1, DP, lambda k: pl.semaphore_signal(barrier, inc=1, device_id=(to_dp(k), ep), device_id_type=MESH))
    loop(1, EP, lambda k: pl.semaphore_signal(barrier, inc=1, device_id=(dp, to_ep(k)), device_id_type=MESH))

    lv = leaving[dp]
    f0 = fresh[0].astype(F32)
    f1 = fresh[1].astype(F32)
    frow = jnp.sum(jnp.where(iota(f1.shape, 0) == lv, f1, 0.0), axis=0, keepdims=True)
    frow = jnp.concatenate([frow, jnp.zeros((1, 640 - LW), F32)], axis=1)
    fpieces = [frow[:, 128 * i : 128 * (i + 1)] for i in range(5)]
    loads[0].wait()
    a1s[0:LW, 0:HEADS] = q2v[lv]
    a1s[LW : LW + 16] = jnp.concatenate(fpieces + [jnp.zeros((11, 128), F32)], axis=0).astype(BF)
    a1s[LW + 16 :] = jnp.zeros((a1s.shape[0] - LW - 16, 128), BF)
    mine = pl.ds(pl.multiple_of(ep * PIECE, 16), PIECE)
    a1r[core, z] = a1s[mine]
    pl.semaphore_wait(barrier, DP + EP - 2)

    def spread_z(src, dst, s, r):
        def copy(i):
            t = (z + i) % NZ
            return remote(src(t), dst(z), s.at[t], r.at[z], t * 2 + core, ep)

        def arrive(i):
            t = (z + NZ - i) % NZ
            return remote(src(t), dst(t), s.at[t], r.at[t], t * 2 + core, ep)

        return Exchange(moves, 1, NZ, copy, arrive)

    a1 = spread_z(lambda t: a1s.at[mine], lambda t: a1r.at[core, t], sa1, ra1)
    a1.start()
    for c in loads[1:6] + pairs + loads[6:]:
        c.start()

    near = DP // 5
    ow_x = [
        spread_dp(lo, hi, lambda d: ow_h.at[:, window(d)], lambda d: owr.at[d], sow, row_)
        for lo, hi in ((1, 1 + near), (DP - near, DP), (1 + near, DP - near))
    ]
    ow_x[0].start()
    ow_x[1].start()

    def attend(q, s, live_fresh, fkeys):
        kt = cv[s]
        score = dot(q, kt, 0, 0) * SCORE_SCALE
        pos = ep * T + iota(score.shape, 1)
        live = pos < lengths[dp * SL + s]
        fscore = dot(q, fkeys, 0, 1) * SCORE_SCALE
        score = jnp.where(live, score, MASKED)
        fscore = jnp.where(live_fresh, fscore, MASKED)
        peak = jnp.maximum(
            jnp.max(score, axis=1, keepdims=True), jnp.max(fscore, axis=1, keepdims=True)
        )
        w = jnp.where(live, jnp.exp(score - peak), 0.0)
        fw = jnp.where(live_fresh, jnp.exp(fscore - peak), 0.0)
        total = jnp.sum(w, axis=1, keepdims=True) + jnp.sum(fw, axis=1, keepdims=True)
        v = dot(w.astype(BF), kt[:LAT], 1, 1) + dot(fw.astype(BF), fkeys[:, :LAT])
        return peak, total, v

    group = iota((HEADS, 128), 1) >> 4

    def attend_step(k, query_of, live_of):
        stat = jnp.zeros((HEADS, 128), F32)
        for p in range(SL // 2):
            both = []
            for s in (2 * p, 2 * p + 1):
                peak, total, v = attend(query_of(s), s, live_of(s), fk[...])
                stat = jnp.where(group == 2 * s, peak, jnp.where(group == 2 * s + 1, total, stat))
                both.append(v.reshape(EP, HP, LAT))
            bs[k, :, 16 * p : 16 * p + 16, :] = jnp.concatenate(both, axis=1).astype(BF)
        bt[k] = stat.reshape(EP, HP, 128)

    def keep_own(k):
        br[k, ep] = bs[k, ep]
        btr[k, ep] = bt[k, ep]

    def partial_exchange(k):
        return (
            spread_ep(1, EP, lambda e: bt.at[k, e], lambda e: btr.at[k, e], st.at[k], rt.at[k]),
            spread_ep(1, EP, lambda e: bs.at[k, e], lambda e: br.at[k, e], sb.at[k], rb.at[k]),
        )

    b_x = [partial_exchange(0), partial_exchange(1)]

    fcol = iota((1, 16), 1)
    at_zero = ep == 0
    fk[...] = jnp.concatenate([f0, f1, jnp.zeros((8, LW), F32)], axis=0).astype(BF)
    loads[1].wait()
    for s in range(SL):
        loads[2 + s].wait()
    attend_step(0, lambda s: q1v[s], lambda s: (fcol == s) & at_zero)
    keep_own(0)

    a1.wait()
    a1c = Exchange(
        moves, 0, 1,
        lambda i: remote(a1r.at[core], a1r.at[core], sa1c, ra1c, sibling, ep),
        lambda i: remote(a1r.at[1 - core], a1r.at[1 - core], sa1c, ra1c, sibling, ep),
    )
    a1c.start()
    a1c.wait()
    ow_x[2].start()
    other = target[dp]
    piece = a1r[other & 1, other >> 1]
    a2s[...] = piece
    a2r[mine] = piece

    def piece_rows(e):
        return a2r.at[pl.ds(pl.multiple_of(e * PIECE, 16), PIECE)]

    a2 = spread_ep(1, EP, lambda e: a2s, piece_rows, sa2, ra2)
    a2.start()
    for x in b_x[0]:
        x.start()

    row = iota((ROWS, 2 * SL * DP), 0)
    col = iota((ROWS, 2 * SL * DP), 1)
    half_bits = HALF.bit_length() - 1
    r_core = row >> half_bits
    r_z = (row >> 3) & (NZ - 1)
    r_step = (row >> 2) & 1
    slot = (r_z * 2 + r_core) * SL + (row & 3)
    held = slot
    for r in range(DP):
        t = target[r]
        held = jnp.where(slot == t * SL + leaving[t], r * SL + leaving[r], held)
    held = jnp.where(r_step == 1, held, slot)
    place = ((held >> 2) * 8 + r_step * 4 + (held & 3)) == col
    code = codes[...].astype(F32)
    share = code / jnp.sum(code, axis=1, keepdims=True) * ROUTE_SCALE
    weight = jnp.sum(jnp.where(ids[...] == ep, share, 0.0), axis=1)
    weight = jnp.concatenate([weight[0:1], weight[1:2]], axis=1)
    own_place = (r_step * (SL * DP) + slot) == col
    rw[...] = jnp.broadcast_to(
        jnp.sum(jnp.where(own_place, weight, 0.0), axis=1, keepdims=True), (ROWS, 128)
    )
    place = jnp.where(place, 1.0, 0.0).astype(BF)
    lines = 2 * BW // 128
    seven = jnp.zeros((lines, 128), F32)
    mixed_gain = jnp.zeros((lines, 128), F32)
    for i in range(EP // 2):
        seven = jnp.where(dp // 2 == i, gain[lines * i : lines * (i + 1)], seven)
        mixed_gain = jnp.where(ep // 2 == i, gain[lines * i : lines * (i + 1)], mixed_gain)
    seven = jnp.concatenate([seven[i : i + 1] for i in range(lines)], axis=1)
    mixed_gain = jnp.concatenate([mixed_gain[i : i + 1] for i in range(lines)], axis=1)
    mixed_gain = jnp.where(ep % 2 == 1, mixed_gain[:, BW:], mixed_gain[:, :BW])

    def quarter(wide):
        out = wide[:, :HB]
        for i in range(1, 4):
            out = jnp.where((dp % 2) * 2 + col_half == i, wide[:, HB * i : HB * (i + 1)], out)
        return out

    own_gain = quarter(seven)
    loads[6].wait()
    wide = rv[...].astype(F32)
    own_resid = [
        jnp.where(first_core == 0, wide[k, 8 * t : 8 * t + 4], wide[k, 8 * t + 4 : 8 * t + 8])
        for t in range(2)
        for k in range(2)
    ]
    own_resid = quarter(jnp.concatenate(own_resid, axis=0))

    attend_step(1, lambda s: q2v[s], lambda s: ((fcol == s) | (fcol == 4 + s)) & at_zero)
    a2.wait()
    moved_f = a2r[LW : LW + 16].astype(F32)
    moved_f = jnp.concatenate([moved_f[i : i + 1] for i in range(5)], axis=1)[:, :LW]
    fkeys = jnp.concatenate([f0, f1, moved_f, jnp.zeros((7, LW), F32)], axis=0).astype(BF)
    peak, total, v = attend(
        a2r[0:LW, 0:HEADS], lv, ((fcol == lv) | (fcol == 8)) & at_zero, fkeys
    )
    v = v.reshape(EP, HP, LAT)
    twice = jnp.concatenate([v, v], axis=1)
    upper = iota(twice.shape, 1) >> 3
    for p in range(SL // 2):
        rows = bs[1, :, 16 * p : 16 * p + 16, :].astype(F32)
        bs[1, :, 16 * p : 16 * p + 16, :] = jnp.where(upper + 2 * p == lv, twice, rows).astype(BF)
    stat = bt[1].reshape(HEADS, 128)
    stat = jnp.where(group == 2 * lv, peak, jnp.where(group == 2 * lv + 1, total, stat))
    bt[1] = stat.reshape(EP, HP, 128)
    keep_own(1)
    for x in b_x[1]:
        x.start()

    head_of = iota((SL * HP, VD), 0) & (HP - 1)

    c_x = [
        spread_dp(1, DP, lambda d, k=k: cs.at[k], lambda d, k=k: cr.at[k, d], scs.at[k], rcs.at[k])
        for k in range(2)
    ]

    def merge(k):
        for x in b_x[k]:
            x.wait()
        stats = btr[k]
        w = jnp.exp(stats - jnp.max(stats, axis=0, keepdims=True))
        shifted = jnp.concatenate([stats[:, :, 16:], stats[:, :, :16]], axis=2)
        sc[...] = w / jnp.sum(w * shifted, axis=0, keepdims=True)

        def add(j, acc):
            one = sc[j]
            scale = jnp.concatenate([one[:, 32 * s : 32 * s + 1] for s in range(SL)], axis=0)
            return acc + scale * br[k, j].astype(F32)

        latent = lax.fori_loop(0, EP, add, jnp.zeros((SL * HP, LAT), F32)).astype(BF)
        values = jnp.zeros((SL * HP, VD), F32)
        for p in range(HP // 2):
            two = dot(latent, vw[p])
            values = jnp.where(head_of == 2 * p, two[:, :VD], values)
            values = jnp.where(head_of == 2 * p + 1, two[:, VD:], values)
        values = values.astype(BF)
        flat = []
        for h in range(HP):
            want = iota((SL, SL * HP), 0) * HP + h
            flat.append(dot(jnp.where(iota((SL, SL * HP), 1) == want, 1.0, 0.0).astype(BF), values))
        few = HP // 4
        flat = [jnp.concatenate(flat[few * t : few * (t + 1)], axis=1) for t in range(4)]
        flat = jnp.concatenate(flat, axis=0).astype(BF)
        cs[k] = flat
        cr[k, dp] = flat
        c_x[k].start()

    for c in pairs:
        c.wait()
    merge(0)
    merge(1)

    loads[9].wait()
    for move in ow_x:
        move.wait()
    for h in range(HP):
        lines_of = [owr[d, VC * h : VC * (h + 1)].astype(F32) for d in range(DP)]
        owp[VD * h : VD * (h + 1)] = jnp.concatenate(lines_of, axis=0).astype(BF)

    own_rows = pl.ds(pl.multiple_of(core * HALF, 16), HALF)
    other_rows = pl.ds(pl.multiple_of((1 - core) * HALF, 16), HALF)
    odd = dp % 2 == 1

    def own_columns(part):
        return jnp.where(odd, part[:, WIN - BW :], part[:, :BW])

    came = []
    for k in range(2):
        c_x[k].wait()
        one = cr[k].astype(F32)
        came.append(jnp.concatenate([one[:, SL * t : SL * (t + 1)] for t in range(4)], axis=2))
    came = jnp.concatenate(came, axis=1).reshape(ROWS, HP * VD)
    came = dot(place, came.astype(BF)).astype(BF)
    part = own_columns(dot(came, owp[...])).astype(BF)
    for g in range(EP // 2):
        for t in range(2):
            es1[2 * g + t] = part[16 * g : 16 * (g + 1), HB * t : HB * (t + 1)]
    er1[ep] = es1[ep]
    e_x = spread_ep(1, EP, lambda e: es1.at[e], lambda e: er1.at[e], s1, r1)
    e_x.start()
    e_x.wait()
    hidden = own_resid + jnp.sum(er1[...].astype(F32), axis=0)

    scaled = hidden * own_gain
    square = jnp.sum(hidden * hidden, axis=1, keepdims=True)
    hi = square.astype(BF).astype(F32)
    mid = (square - hi).astype(BF).astype(F32)
    lane = iota((16, 256 - HB), 1)
    extra = jnp.where(lane == 0, hi, jnp.where(lane == 1, mid, square - hi - mid))
    block = jnp.concatenate([scaled, extra], axis=1).astype(BF)
    gs[...] = block

    def rows_of(e):
        return pl.ds(pl.multiple_of((e // 2) * 16, 16), 16)

    hb[core, col_half, z, rows_of(ep)] = block
    gz_x = spread_z(lambda t: gs, lambda t: hb.at[core, col_half, t, rows_of(ep)], sgz, rgz)
    gz_x.start()
    gz_x.wait()

    def region(e, c):
        return hb.at[c, e % 2, :, rows_of(e)]

    def region_half(e, h):
        return hb.at[core, e % 2, pl.ds(h * (NZ // 2), NZ // 2), rows_of(e)]

    NX = 4 if EP == 16 else 2
    NY = EP // NX
    y, x = ep // NX, ep % NX

    def on_x(i):
        return y * NX + (x + i) % NX

    def on_y(i):
        return ((y + i) % NY) * NX + x

    def whole(e):
        return remote(region(ep, core), region(ep, core), sgx.at[e], rgx.at[ep], dp, e)

    def whole_wait(e):
        remote(region(e, core), region(e, core), sgx.at[e], rgx.at[e], dp, e).wait_recv()

    def first_on(i, j):
        e = on_x(NX - i)
        half = region_half(e, 0)
        return remote(half, half, sga.at[i, j], rga.at[e], dp, on_y(j))

    def second_on(i, j):
        e = on_y(NY - i)
        half = region_half(e, 1)
        return remote(half, half, sgb.at[i, j], rgb.at[e], dp, on_x(j))

    def gc_copy(e):
        return remote(region(e, core), region(e, core), sgc.at[e], rgc.at[e], sibling, ep)

    def gc_wait(e):
        other = region(e, 1 - core)
        remote(other, other, sgc.at[e], rgc.at[e], sibling, ep).wait_recv()

    loop(1, NX, lambda i: whole(on_x(i)).start())
    loop(1, NY, lambda i: whole(on_y(i)).start())
    gc_copy(ep).start()
    loads[7].wait()
    loads[8].wait()

    def pass_x(i):
        whole_wait(on_x(NX - i))
        loop(1, NY, lambda j: first_on(i, j).start())
        gc_copy(on_x(NX - i)).start()

    def pass_y(i):
        whole_wait(on_y(NY - i))
        loop(1, NX, lambda j: second_on(i, j).start())
        gc_copy(on_y(NY - i)).start()

    def across(n):
        e = ((y + 1 + n // (NX - 1)) % NY) * NX + (x + 1 + n % (NX - 1)) % NX
        first, second = region_half(e, 0), region_half(e, 1)
        remote(first, first, sga.at[0, 0], rga.at[e], dp, e).wait_recv()
        remote(second, second, sgb.at[0, 0], rgb.at[e], dp, e).wait_recv()
        gc_copy(e).start()

    for i in range(1, max(NX, NY)):
        if i < NX:
            pass_x(i)
        if i < NY:
            pass_y(i)
    loop(0, (NX - 1) * (NY - 1), across)

    def project(t, acc):
        proj, squares = acc
        for c in range(2):
            for half in range(2):
                block = hb[c, half, t]
                w = gu[pl.ds(pl.multiple_of((2 * t + c) * BW + half * HB, 16), HB), :]
                proj = proj + dot(block[:, :HB], w)
                squares = squares + block[:, 128:].astype(F32)
        return proj, squares

    loop(0, EP, gc_wait)
    acc = (jnp.zeros((ROWS, 256), F32), jnp.zeros((ROWS, 128), F32))
    proj, squares = lax.fori_loop(0, NZ, project, acc)
    at = pl.ds(pl.multiple_of((core * NZ + z) // 2 * 16, 16), 16)
    sixteen = jnp.concatenate(
        [hb[ep % 2, t, ep // 2, at, :].astype(F32)[:, :HB] for t in range(2)], axis=1
    )
    hidden = jnp.where(z % 2 == 1, sixteen[8:], sixteen[:8]) / mixed_gain
    off = HB - 128
    square = squares[:, off : off + 1] + squares[:, off + 1 : off + 2] + squares[:, off + 2 : off + 3]
    scale = lax.rsqrt(square / float(BW * EP) + NORM_EPS)
    g = proj[:, :128] * scale
    u = proj[:, 128:] * scale
    act = (g / (1.0 + jnp.exp(-g)) * u * rw[:, 0:1]).astype(BF)
    loads[10].wait()

    def c_copy(j):
        return remote(pc.at[j, other_rows], pr.at[j], s2c.at[j], r2c.at[j], sibling, ep)

    def x_copy(j):
        return remote(xs.at[j], xr.at[ep], s2x.at[j], r2x.at[ep], dp, j)

    def pair(i):
        return (ep // 2 + 1 + i) % (EP // 2)

    def first(i):
        jp = pair(i)
        part = dot(act, dn[:, pl.ds(pl.multiple_of(jp * 2 * BW, 128), 2 * BW)])
        pc[2 * jp] = part[:, :BW].astype(BF)
        pc[2 * jp + 1] = part[:, BW:].astype(BF)
        c_copy(2 * jp).start()
        c_copy(2 * jp + 1).start()

    def second(i):
        for t in range(2):
            j = 2 * pair(i) + t
            c_copy(j).wait_recv()
            part = pc[j, own_rows].astype(F32) + pr[j].astype(F32)
            tail = part[:, BW - 64 :]
            tail = jnp.concatenate([tail[: HALF // 2], tail[HALF // 2 :]], axis=1)
            tiles = [part[:, 128 * i : 128 * (i + 1)] for i in range(BW // 128)]
            xs[j] = jnp.concatenate(tiles + [tail], axis=0).astype(BF)

            @pl.when(j != ep)
            def _():
                x_copy(j).start()

    def both(i):
        first(i)
        second(i - 1)

    first(0)
    loop(1, EP // 2, both)
    second(EP // 2 - 1)

    def x_sum(i, acc):
        j = to_ep(EP - i)
        remote(xs.at[j], xr.at[j], s2x.at[j], r2x.at[j], dp, j).wait_recv()
        return acc + xr[j].astype(F32)

    total = lax.fori_loop(1, EP, x_sum, xs[ep].astype(F32))
    tail = total[HALF * (BW // 128) :]
    tail = jnp.concatenate([tail[:, :64], tail[:, 64:]], axis=0)
    tiles = [total[HALF * i : HALF * (i + 1)] for i in range(BW // 128)]
    total = jnp.concatenate(tiles + [tail], axis=1).reshape(NZ, 8, BW)
    zs[...] = jnp.concatenate([total[:, :, :HB], total[:, :, HB:]], axis=1).astype(BF)
    zr[z] = zs[z]
    z_x = spread_z(lambda t: zs.at[t], lambda t: zr.at[t], s2z, r2z)
    z_x.start()
    z_x.wait()
    total = jnp.sum(zr[...].astype(F32), axis=0)
    routed = jnp.concatenate([total[:8], total[8:]], axis=1)
    mixed = (hidden + routed).astype(out.dtype)
    out[0] = mixed[0:4]
    out[1] = mixed[4:8]

    for move in moves:
        move.finish()
    loop(1, NX, lambda i: whole(on_x(i)).wait_send())
    loop(1, NY, lambda i: whole(on_y(i)).wait_send())
    for i in range(1, NX):
        loop(1, NY, lambda j: first_on(i, j).wait_send())
    for i in range(1, NY):
        loop(1, NX, lambda j: second_on(i, j).wait_send())
    loop(0, EP, lambda e: gc_copy(e).wait_send())
    loop(0, EP, lambda j: c_copy(j).wait_send())
    loop(1, EP, lambda i: x_copy(to_ep(i)).wait_send())


def body(
    DP, EP,
    latent_cache, lengths, queries, fresh_latent, leaving, target, value_weight, output_weight,
    residual_stream, norm_gain, expert_ids, gate_codes, gate_weight, up_weight, down_weight,
):
    SL, T, LW = latent_cache.shape
    H = queries.shape[2]
    HP, _, VD = value_weight.shape
    D = norm_gain.shape[0]
    BW = D // EP
    NZ = DP // 2
    ROWS = DP * 8
    HALF = ROWS // 2
    PIECE = 768 // EP
    cache = jnp.swapaxes(latent_cache, 1, 2)
    q = jnp.swapaxes(queries, 2, 3)
    gain = norm_gain.astype(F32).reshape(D // 128, 128)
    ow = output_weight.reshape(HP * output_weight.shape[1], D)
    smem = pl.BlockSpec(memory_space=pltpu.SMEM)
    vmem = pl.BlockSpec(memory_space=pltpu.VMEM)
    anyw = pl.BlockSpec(memory_space=pl.ANY)
    V = pltpu.VMEM
    sems = lambda *n: pltpu.SemaphoreType.DMA(n)
    scratch = [
        V((SL, LW, H), BF), V((SL, LW, H), BF), V((SL, LW, T), BF), V((HP // 2, value_weight.shape[1], 2 * VD), BF),
        V((D, 256), BF), V((2, 16, 2 * BW), BF),
        V((DP, ow.shape[0], BW + 64), BF),
        V((HP * VD, BW + 64), BF), V((128, D), BF),
        V((768, 128), BF), V((2, NZ, PIECE, 128), BF), V((PIECE, 128), BF), V((768, 128), BF), V((16, LW), BF),
        V((2, EP, SL * HP, LAT), BF), V((2, EP, HP, 128), F32), V((2, EP, SL * HP, LAT), BF),
        V((2, EP, HP, 128), F32), V((EP, HP, 128), F32), V((SL * HP, LAT), BF),
        V((2, 16, HP * VD // 4), BF), V((2, DP, 16, HP * VD // 4), BF),
        *[V((EP, 16, BW // 2), BF)] * 2,
        V((EP, ROWS, BW), BF), V((EP, HALF, BW), BF), *[V((EP, HALF * BW // 128, 128), BF)] * 2, *[V((NZ, 16, BW // 2), BF)] * 2,
        V((16, 256), BF), V((2, 2, NZ, ROWS, 256), BF), V((ROWS, 128), F32),
        sems(12 + HP), sems(NZ), sems(NZ), pltpu.SemaphoreType.DMA, pltpu.SemaphoreType.DMA, sems(EP), sems(EP), sems(2, EP), sems(2, EP), sems(2, EP), sems(2, EP),
        sems(2, DP), sems(2, DP),
        sems(DP), sems(DP), *[sems(EP)] * 2, *[sems(EP)] * 4, *[sems(NZ)] * 2,
        sems(NZ), sems(NZ), sems(EP), sems(EP), sems(EP), sems(EP), sems(4, 4), sems(EP), sems(4, 4), sems(EP),
    ]
    return pl.pallas_call(
        functools.partial(kernel, DP, EP),
        out_shape=jax.ShapeDtypeStruct((2, SL, BW), BF),
        in_specs=[smem] * 3 + [vmem] * 4 + [anyw] * 8,
        out_specs=vmem,
        scratch_shapes=scratch,
        compiler_params=pltpu.CompilerParams(
            collective_id=0, has_side_effects=True, vmem_limit_bytes=56 * 2**20
        ),
        name="decode",
    )(
        lengths, leaving, target, fresh_latent,
        jnp.swapaxes(expert_ids, 1, 2), jnp.swapaxes(gate_codes, 1, 2), gain, residual_stream,
        cache, q, value_weight, ow, gate_weight[0], up_weight[0], down_weight[0],
    )


def solution(mesh):
    placed = (
        P("dp", "ep", None), P(), P(None, "dp", None, None), P(None, "dp", None), P(), P(),
        P("ep", None, None), P("ep", "dp", None), P(), P(), P(), P(),
        P("ep", None, "dp"), P("ep", None, "dp"), P("ep", "dp", None),
    )
    return jax.shard_map(
        functools.partial(body, mesh.shape["dp"], mesh.shape["ep"]),
        mesh=mesh, in_specs=placed, out_specs=P(None, "dp", "ep"), check_vma=False,
    )
```
